32 devices in a mesh: dev: 32 (over z, y, x, core).
Axes of the slice: x: 2, y: 2, z: 4, core: 2. Of those that a mesh axis runs over, the one named last changes fastest.
Arguments:
- tokens: bfloat16 [8192, 2048], P('dev'), may hold values from -6 to 6
- cotangent: bfloat16 [8192, 2048], P('dev'), may hold values from -6 to 6
- segment_ids: int32 [8192], replicated, may hold values from 0 to 14, as said below
- piece_ids: int32 [8192], replicated, may hold values from 0 to 15, as said below
- w_query: float32 [2048, 2048], P('dev'), may hold values from -0.125 to 0.125
- w_key: float32 [2048, 2048], P('dev'), may hold values from -0.125 to 0.125
- w_value: float32 [2048, 2048], P('dev'), may hold values from -0.125 to 0.125
- w_out: float32 [2048, 2048], P('dev'), may hold values from -0.125 to 0.125
- query_gain: float32 [2048], P('dev'), may hold values from 0.1 to 1.9
- key_gain: float32 [2048], P('dev'), may hold values from 0.1 to 1.9
- mixer_gain: float32 [2048], P('dev'), may hold values from 0.1 to 1.9
- w_gate: float32 [2048, 8192], P('dev'), may hold values from -0.125 to 0.125
- w_up: float32 [2048, 8192], P('dev'), may hold values from -0.125 to 0.125
- w_down: float32 [8192, 2048], P('dev'), may hold values from -0.0625 to 0.0625
- feed_gain: float32 [2048], P('dev'), may hold values from 0.1 to 1.9
Outputs:
- out_tokens: bfloat16 [8192, 2048], P('dev')
- g_tokens: float32 [8192, 2048], P('dev')
- g_w_query: float32 [2048, 2048], P('dev')
- g_w_key: float32 [2048, 2048], P('dev')
- g_w_value: float32 [2048, 2048], P('dev')
- g_w_out: float32 [2048, 2048], P('dev')
- g_query_gain: float32 [2048], P('dev')
- g_key_gain: float32 [2048], P('dev')
- g_mixer_gain: float32 [2048], P('dev')
- g_w_gate: float32 [2048, 8192], P('dev')
- g_w_up: float32 [2048, 8192], P('dev')
- g_w_down: float32 [8192, 2048], P('dev')
- g_feed_gain: float32 [2048], P('dev')
The draws below stay inside these ranges and needn't reach their ends.
Inputs may be any that keep to these rules, and one draw needn't show every extreme that they name: `segment_ids`: starts at 0, never falls, rises by one at each new sequence; no sequence crosses a multiple of 1024 tokens; the first sequence holds exactly 1024 tokens, and each following aligned run of 1024 tokens holds exactly two sequences of 256 tokens or more. `piece_ids`: 0 marks text; value s + 1 marks the picture piece of sequence s, one run of exactly 256 tokens inside that sequence; a sequence has at most one piece, and the first and the last sequence have one.
All inputs are finite; a program needn't handle non-finite values.
Results may differ from the reference program's by a relative error of at most 0.015.
The reference program's roundings to bfloat16 on the way count: a program that leaves them out, or rounds other values in their place, can miss the bound.
Values may be sent and summed in bfloat16 or wider, within the bound.
No kernel may reach another device: no remote copies, remote signals or barrier semaphores. Data moves between devices by JAX's collectives and lax.ppermute only.
A program may use at most 512 MiB of HBM per device.

```python
import math
import jax
import jax.numpy as jnp
from jax import lax

D = 2048
HEADS = 16
HEAD = 128
FF = 8192
SEQ_MAX = 1024
PIECE = 256
TOKENS = 8192


def layout(key):
    block_count = TOKENS // SEQ_MAX
    segment_count = 2 * block_count - 1
    subkeys = jax.random.split(jax.random.fold_in(key, 11), 3)
    cuts = jax.random.randint(subkeys[0], (block_count,), PIECE, SEQ_MAX - PIECE + 1).astype(jnp.int32)
    numbers = jnp.arange(segment_count, dtype=jnp.int32)
    owner_block = (numbers + 1) // 2
    second_half = (numbers % 2 == 0) & (numbers > 0)
    cut_of = cuts[owner_block]
    starts = jnp.where(numbers == 0, 0, owner_block * SEQ_MAX + jnp.where(second_half, cut_of, 0)).astype(jnp.int32)
    lengths = jnp.where(numbers == 0, SEQ_MAX, jnp.where(second_half, SEQ_MAX - cut_of, cut_of)).astype(jnp.int32)
    places = jnp.arange(TOKENS, dtype=jnp.int32)
    block_of = places // SEQ_MAX
    offset_of = places % SEQ_MAX
    segment = jnp.where(block_of == 0, 0, 2 * block_of - 1 + (offset_of >= cuts[block_of]).astype(jnp.int32)).astype(jnp.int32)
    shifts = jax.random.randint(subkeys[1], (segment_count,), 0, lengths - PIECE + 1).astype(jnp.int32)
    with_piece = jax.random.randint(subkeys[2], (segment_count,), 0, 2)
    with_piece = jnp.where((numbers == 0) | (numbers == segment_count - 1), 1, with_piece)
    opening = (starts + shifts)[segment]
    inside = (places >= opening) & (places < opening + PIECE) & (with_piece[segment] == 1)
    piece_of = jnp.where(inside, segment + 1, 0)
    return (segment.astype(jnp.int32), piece_of.astype(jnp.int32))


def draw_segment_ids(key, part):
    return layout(key)[0]


def draw_piece_ids(key, part):
    return layout(key)[1]


def spiked(values, rng, source, target, blocks, factor):
    def block_of(dim):
        return (jnp.arange(values.shape[dim]) // (values.shape[dim] // blocks)).reshape((-1,) + (1,) * (values.ndim - 1 - dim))

    one_side = jax.random.permutation(rng, blocks)[block_of(target)]
    other_side = (block_of(target) + blocks // 2) % blocks
    return jnp.where((block_of(source) == one_side) | (block_of(source) == other_side), factor * values, values)


def steps_of(key, dims, pieces, smallest, largest):
    loudness = 1.0
    for position, blocks in pieces:
        steps = jax.random.uniform(jax.random.fold_in(jax.random.fold_in(key, 6), position), (blocks,), jnp.float32, smallest / len(pieces), largest / len(pieces))
        loudness = loudness * jnp.repeat(jnp.exp(steps), dims[position] // blocks).reshape((-1,) + (1,) * (len(dims) - 1 - position))
    return loudness


def normal_values(stream_key, extent, spread, most, shards=(), held_as=jnp.bfloat16):
    values = spread * jax.random.normal(stream_key, extent, jnp.float32)
    if shards:
        values = values * steps_of(stream_key, extent, shards, -0.22, 0.18)
    return jnp.clip(values, -most, most).astype(held_as)


def bell_draw_with(stream_key, extent, spread, reach, pieces, heavy, kind=jnp.bfloat16):
    array = spread * jax.random.normal(stream_key, extent, jnp.float32)
    if pieces:
        array = array * steps_of(stream_key, extent, pieces, -0.22, 0.18)
    return jnp.clip(spiked(array, jax.random.fold_in(stream_key, 3), *heavy), -reach, reach).astype(kind)


def setup_inputs(seed: int = 0) -> dict:
    keys = jax.random.split(jax.random.key(seed), 16)
    tokens = bell_draw_with(keys[0], (TOKENS, D), 1.0, 6.0, ((0, 32),), (0, 1, 32, 2.75))
    cotangent = bell_draw_with(keys[1], (TOKENS, D), 1.0, 6.0, ((0, 32),), (0, 1, 32, 2.75))
    segment_ids = draw_segment_ids(jax.random.fold_in(keys[15], 71), 0)
    piece_ids = draw_piece_ids(jax.random.fold_in(keys[15], 71), 0)
    w_query = normal_values(keys[4], (D, D), D ** -0.5, 0.125, ((0, 32),), jnp.float32)
    w_key = normal_values(keys[5], (D, D), D ** -0.5, 0.125, ((0, 32),), jnp.float32)
    w_value = normal_values(keys[6], (D, D), D ** -0.5, 0.125, ((0, 32),), jnp.float32)
    w_out = normal_values(keys[7], (D, D), D ** -0.5, 0.125, ((0, 32),), jnp.float32)
    query_gain = jnp.clip(1.0 + 0.18 * jax.random.normal(keys[8], (D,), jnp.float32), 0.1, 1.9)
    key_gain = jnp.clip(1.0 + 0.18 * jax.random.normal(keys[9], (D,), jnp.float32), 0.1, 1.9)
    mixer_gain = jnp.clip(1.0 + 0.18 * jax.random.normal(keys[10], (D,), jnp.float32), 0.1, 1.9)
    w_gate = normal_values(keys[11], (D, FF), D ** -0.5, 0.125, ((0, 32),), jnp.float32)
    w_up = normal_values(keys[12], (D, FF), D ** -0.5, 0.125, ((0, 32),), jnp.float32)
    w_down = normal_values(keys[13], (FF, D), FF ** -0.5, 0.0625, ((0, 32),), jnp.float32)
    feed_gain = jnp.clip(1.0 + 0.18 * jax.random.normal(keys[14], (D,), jnp.float32), 0.1, 1.9)
    return dict(tokens=tokens, cotangent=cotangent, segment_ids=segment_ids, piece_ids=piece_ids, w_query=w_query, w_key=w_key, w_value=w_value, w_out=w_out, query_gain=query_gain, key_gain=key_gain, mixer_gain=mixer_gain, w_gate=w_gate, w_up=w_up, w_down=w_down, feed_gain=feed_gain)


NORM_EPS = 1e-06
ROPE_BASE = 500000.0
MASKED = -1e+30

@jax.custom_vjp
def low(v):
    return lax.optimization_barrier(v.astype(jnp.bfloat16)).astype(jnp.float32)

@jax.custom_vjp
def low_back(v):
    return v

def low_keep(v):
    return (low(v), None)

def low_pass(kept, grad):
    return (grad,)

def back_keep(v):
    return (v, None)

def back_low(kept, grad):
    return (low(grad),)
low.defvjp(low_keep, low_pass)
low_back.defvjp(back_keep, back_low)

def matmul(left, right):
    return jnp.dot(left, right, precision=lax.Precision.HIGHEST, preferred_element_type=jnp.float32)

def rms_norm(values, norm_gain):
    return values * lax.rsqrt(lax.optimization_barrier(jnp.mean(values * values, axis=-1, keepdims=True)) + NORM_EPS) * norm_gain

def segment_positions(segment_ids):
    places = jnp.arange(segment_ids.shape[0], dtype=jnp.int32)
    opens = jnp.concatenate([jnp.ones((1,), bool), segment_ids[1:] != segment_ids[:-1]])
    starts = lax.cummax(jnp.where(opens, places, 0).astype(jnp.int32), axis=0)
    return places - starts

def rope_tables(positions):
    freqs = jnp.exp(jnp.arange(HEAD // 2, dtype=jnp.float32) * (-2.0 * math.log(ROPE_BASE) / HEAD))
    angles = positions.astype(jnp.float32)[:, None] * freqs[None, :]
    return (jnp.cos(angles), jnp.sin(angles))

def rotate(values, cosine, sine_table):
    row_count = values.shape[0]
    shaped = values.reshape(row_count, HEADS, HEAD)
    first_half = shaped[:, :, :HEAD // 2]
    second_half = shaped[:, :, HEAD // 2:]
    cos_rows = cosine[:, None, :]
    sin_rows = sine_table[:, None, :]
    turned = jnp.concatenate([first_half * cos_rows - second_half * sin_rows, second_half * cos_rows + first_half * sin_rows], axis=-1)
    return turned.reshape(row_count, HEADS * HEAD)

def attention(query_rot, key_rot, value_low, segment_ids, piece_ids):
    span = SEQ_MAX
    block_count = query_rot.shape[0] // span
    pad_key = jnp.pad(key_rot, ((span, span), (0, 0)))
    pad_value = jnp.pad(value_low, ((span, span), (0, 0)))
    pad_segment = jnp.pad(segment_ids, (span, span), constant_values=-1)
    pad_piece = jnp.pad(piece_ids, (span, span))

    def one_block(index):
        start = (index * span).astype(jnp.int32)
        query_rows = lax.dynamic_slice_in_dim(query_rot, start, span, 0).reshape(span, HEADS, HEAD)
        key_rows = lax.dynamic_slice_in_dim(pad_key, start, 3 * span, 0).reshape(3 * span, HEADS, HEAD)
        value_rows = lax.dynamic_slice_in_dim(pad_value, start, 3 * span, 0).reshape(3 * span, HEADS, HEAD)
        segment_query = lax.dynamic_slice_in_dim(segment_ids, start, span, 0)
        piece_query = lax.dynamic_slice_in_dim(piece_ids, start, span, 0)
        segment_key = lax.dynamic_slice_in_dim(pad_segment, start, 3 * span, 0)
        piece_key = lax.dynamic_slice_in_dim(pad_piece, start, 3 * span, 0)
        query_place = start + jnp.arange(span, dtype=jnp.int32)
        key_place = start - span + jnp.arange(3 * span, dtype=jnp.int32)
        visible = (segment_query[:, None] == segment_key[None, :]) & ((key_place[None, :] <= query_place[:, None]) | (piece_query[:, None] == piece_key[None, :]) & (piece_query[:, None] > 0))
        scores = low_back(jnp.einsum('qhd,khd->hqk', query_rows, key_rows, precision=lax.Precision.HIGHEST) * HEAD ** (-0.5))
        masked = jnp.where(visible[None], scores, MASKED)
        row_max = lax.optimization_barrier(jnp.max(masked, axis=-1, keepdims=True))
        weights = jnp.exp(masked - row_max)
        softmax_out = weights / lax.optimization_barrier(jnp.sum(weights, axis=-1, keepdims=True))
        mixed = jnp.einsum('hqk,khd->qhd', low(softmax_out), value_rows, precision=lax.Precision.HIGHEST)
        return mixed.reshape(span, HEADS * HEAD)
    blocks = lax.map(jax.checkpoint(one_block), jnp.arange(block_count, dtype=jnp.int32))
    return blocks.reshape(query_rot.shape[0], HEADS * HEAD)

def forward(inputs, params, segment_ids, piece_ids, cosine, sine_table):
    w_query, w_key, w_value, w_out, query_gain, key_gain, mixer_gain, w_gate, w_up, w_down, feed_gain = params
    query = low_back(matmul(inputs, low(w_query)))
    key_proj = low_back(matmul(inputs, low(w_key)))
    value_proj = low(low_back(matmul(inputs, low(w_value))))
    query_rot = low(rotate(rms_norm(query, low(query_gain)), cosine, sine_table))
    key_rot = low(rotate(rms_norm(key_proj, low(key_gain)), cosine, sine_table))
    mixed = low(low_back(attention(query_rot, key_rot, value_proj, segment_ids, piece_ids)))
    branch = low_back(matmul(mixed, low(w_out)))
    hidden_in = inputs + rms_norm(branch, low(mixer_gain))
    hidden_low = low(hidden_in)
    gate_proj = low_back(matmul(hidden_low, low(w_gate)))
    up_proj = low_back(matmul(hidden_low, low(w_up)))
    hidden = low(jax.nn.silu(gate_proj) * up_proj)
    result = low_back(matmul(hidden, low(w_down)))
    return hidden_in + rms_norm(result, low(feed_gain))

def reference(tokens, cotangent, segment_ids, piece_ids, w_query, w_key, w_value, w_out, query_gain, key_gain, mixer_gain, w_gate, w_up, w_down, feed_gain):
    cosine, sine_table = rope_tables(segment_positions(segment_ids))
    inputs = tokens.astype(jnp.float32)
    params = (w_query, w_key, w_value, w_out, query_gain, key_gain, mixer_gain, w_gate, w_up, w_down, feed_gain)

    def apply_layer(values, weights):
        return forward(values, weights, segment_ids, piece_ids, cosine, sine_table)
    result, pullback = jax.vjp(apply_layer, inputs, params)
    g_tokens, grads = pullback(cotangent.astype(jnp.float32))
    return (result.astype(jnp.bfloat16), g_tokens, grads[0], grads[1], grads[2], grads[3], grads[4], grads[5], grads[6], grads[7], grads[8], grads[9], grads[10])
```

```python
import math

import jax
import jax.numpy as jnp
from jax import lax
from jax.sharding import Mesh, PartitionSpec as P

HEAD = 128
SEQ_MAX = 1024
NORM_EPS = 1e-06
ROPE_BASE = 500000.0
MASKED = -1e30
BF16 = jnp.bfloat16
F32 = jnp.float32
GROUP = ("y", "x", "c")
ALL = ("r", "y", "x", "c")


def matmul(left, right):
    return jnp.dot(left, right, preferred_element_type=F32)


def matmul_t(left, right):
    return lax.dot_general(left, right, (((1,), (1,)), ((), ())), preferred_element_type=F32)


def inner_t(left, right):
    return lax.dot_general(left, right, (((0,), (0,)), ((), ())), preferred_element_type=F32)


def inverse_rms(values):
    return lax.rsqrt(jnp.mean(values * values, axis=-1, keepdims=True) + NORM_EPS)


def swap(block, axis):
    return lax.ppermute(block, axis, [(0, 1), (1, 0)])


def group_gather(own):
    half = own.shape[0] // 2
    top, low = own[:half], own[half:]
    top_x = swap(top, "x")
    low_y = swap(low, "y")
    top_y = swap(top, "y")
    low_x = swap(low, "x")
    top_xy = swap(top_x, "y")
    low_xy = swap(low_y, "x")
    chip = jnp.concatenate([own, top_x, low_x, top_y, low_y, top_xy, low_xy], 0)
    parts = [own, jnp.concatenate([top_x, low_y]), jnp.concatenate([top_y, low_x]), jnp.concatenate([top_xy, low_xy])]
    first, second, third, fourth = [swap(part, "c") for part in parts]
    other = jnp.concatenate(
        [
            first,
            second[:half],
            third[half:],
            third[:half],
            second[half:],
            fourth,
        ],
        0,
    )
    return jnp.concatenate([chip, other], 0)


def group_sum(terms):
    total = terms.reshape(terms.shape[0], 2, 2, 2, -1)
    for dim, axis in enumerate(("c", "y", "x")):
        total = total + jnp.flip(swap(total, axis), dim + 1)
    return total.reshape(terms.shape)


def group_scatter(parts, rows):
    width = parts.shape[1]
    half = rows // 2
    low = parts.astype(BF16)
    arrived = swap(low[4 * rows :], "c")
    mine = low[: 4 * rows].astype(F32) + arrived.astype(F32)
    mine = mine.astype(BF16).reshape(2, 2, 2, half, width)
    got_x = swap(mine[:, 1, 0], "x")
    got_y = swap(mine[1, :, 1], "y")
    top = mine[:, 0, 0].astype(F32) + got_x.astype(F32)
    bottom = mine[0, :, 1].astype(F32) + got_y.astype(F32)
    top_last = swap(top[1].astype(BF16), "y")
    bottom_last = swap(bottom[1].astype(BF16), "x")
    return jnp.concatenate([top[0] + top_last.astype(F32), bottom[0] + bottom_last.astype(F32)], 0)


def make_body(inner):
    replicas, per_head = inner
    head_axes = GROUP[3 - int(math.log2(per_head)) :]
    head_groups = 8 // per_head
    own_heads = replicas // per_head

    def body(
        tokens,
        cotangent,
        segment_ids,
        piece_ids,
        w_query,
        w_key,
        w_value,
        w_out,
        query_gain,
        key_gain,
        mixer_gain,
        w_gate,
        w_up,
        w_down,
        feed_gain,
    ):
        rows, width = tokens.shape
        weight_rows = w_query.shape[0]
        unit_rows = w_down.shape[0]
        units = replicas * unit_rows
        columns = own_heads * HEAD
        group_rows = 8 * rows
        blocks = group_rows // SEQ_MAX
        member = lax.axis_index(GROUP)
        replica = lax.axis_index("r")

        def by_head(weight):
            shaped = weight.astype(BF16).reshape(weight_rows, per_head, own_heads, head_groups, HEAD)
            return shaped.transpose(3, 1, 0, 2, 4).reshape(8, weight_rows, columns)

        def by_unit(weight):
            shaped = weight.astype(BF16).reshape(weight_rows, replicas, 8, unit_rows)
            return shaped.transpose(2, 0, 1, 3).reshape(8, weight_rows, units)

        def exchange(parts):
            return lax.all_to_all(parts, GROUP, 0, 0, tiled=True)

        def gather(part):
            return lax.all_gather(part, "r", axis=0, tiled=True)

        qkv_parts = jnp.concatenate([by_head(w_query), by_head(w_key), by_head(w_value)], 2)
        weight_qkv = gather(exchange(qkv_parts).reshape(8 * weight_rows, 3 * columns))
        gate_up_parts = jnp.concatenate([by_unit(w_gate), by_unit(w_up)], 2)
        out_halves = gather(w_out.astype(BF16)).reshape(per_head, own_heads, weight_rows, width)
        out_heads = lax.all_to_all(out_halves, head_axes, 0, 0, tiled=True)
        weight_out = out_heads.transpose(1, 0, 2, 3).reshape(columns, width)
        weight_gate_up = gather(exchange(gate_up_parts).reshape(8 * weight_rows, 2 * units))
        weight_gate, weight_up = weight_gate_up[:, :units], weight_gate_up[:, units:]
        weight_down = gather(w_down.astype(BF16))

        gains = lax.all_gather(
            jnp.stack([query_gain, key_gain, mixer_gain, feed_gain]).astype(BF16), ALL, axis=1, tiled=True
        ).astype(F32)
        head_gains = gains[:2].reshape(2, per_head, own_heads, head_groups, HEAD)
        place = lax.axis_index(head_axes)
        head_group = member // per_head
        head_gains = lax.dynamic_index_in_dim(head_gains, place, 1, keepdims=False)
        head_gains = lax.dynamic_index_in_dim(head_gains, head_group, 2, keepdims=False)
        gain_q, gain_k = head_gains.reshape(2, 1, columns)
        gain_a, gain_f = gains[2:3], gains[3:4]

        orders = [c + 4 * y + 2 * x for c in (0, 1) for y in (0, 1) for x in (0, 1)]
        starts = [(replica * 8 + (member ^ k)) * rows for k in orders]

        def of_group(ids):
            return jnp.concatenate([lax.dynamic_slice_in_dim(ids, s, rows, 0) for s in starts])

        places = jnp.concatenate([s + jnp.arange(rows, dtype=jnp.int32) for s in starts])

        def by_block(array):
            shaped = array.reshape((2, blocks, group_rows // (2 * blocks)) + array.shape[1:])
            return jnp.moveaxis(shaped, 1, 0).reshape((blocks, SEQ_MAX) + array.shape[1:])

        def from_block(array):
            shaped = array.reshape((blocks, 2, SEQ_MAX // 2) + array.shape[2:])
            return jnp.moveaxis(shaped, 0, 1).reshape((group_rows,) + array.shape[2:])

        segment = by_block(of_group(segment_ids))
        piece = by_block(of_group(piece_ids))
        place_block = by_block(places)
        same = segment[:, :, None] == segment[:, None, :]
        visible = same & (
            (place_block[:, None, :] <= place_block[:, :, None])
            | (piece[:, :, None] == piece[:, None, :]) & (piece[:, :, None] > 0)
        )
        before = jnp.sum((segment[:, None, :] < segment[:, :, None]).astype(jnp.int32), -1)
        positions = from_block(place_block % SEQ_MAX - before)
        freqs = jnp.exp(jnp.arange(HEAD // 2, dtype=F32) * (-2.0 * math.log(ROPE_BASE) / HEAD))
        angles = positions.astype(F32)[:, None] * freqs[None, :]
        cosine = jnp.concatenate([jnp.cos(angles), jnp.cos(angles)], 1)[:, None, :]
        sine = jnp.concatenate([-jnp.sin(angles), jnp.sin(angles)], 1)[:, None, :]

        def turned(values, sine_table):
            shaped = values.reshape(group_rows, own_heads, HEAD)
            crossed = jnp.concatenate([shaped[:, :, HEAD // 2 :], shaped[:, :, : HEAD // 2]], -1)
            return (shaped * cosine + crossed * sine_table).reshape(group_rows, columns)

        scale = HEAD ** (-0.5)

        def heads_of(array):
            return by_block(array.reshape(group_rows, own_heads, HEAD))

        group_tokens = group_gather(tokens)
        projected = matmul(group_tokens, weight_qkv)
        query, key, value = jnp.split(projected, 3, axis=1)
        squares = jnp.stack([jnp.sum(query * query, -1), jnp.sum(key * key, -1)])
        squares = group_sum(squares)
        r_q, r_k = lax.rsqrt(squares / width + NORM_EPS)[:, :, None]
        query_rot = turned(query * r_q * gain_q, sine).astype(BF16)
        key_rot = turned(key * r_k * gain_k, sine).astype(BF16)
        q, k, v = heads_of(query_rot), heads_of(key_rot), heads_of(value.astype(BF16))
        scores = jnp.einsum("bqhd,bkhd->bhqk", q, k, preferred_element_type=F32) * scale
        masked = jnp.where(visible[:, None], scores, MASKED)
        row_max = jnp.max(masked, axis=-1, keepdims=True)
        weights = jnp.exp(masked - row_max)
        totals = jnp.sum(weights, axis=-1, keepdims=True)
        softmax = weights / totals
        softmax_low = softmax.astype(BF16)
        mixed = jnp.einsum("bhqk,bkhd->bqhd", softmax_low, v, preferred_element_type=F32)
        mixed_low = from_block(mixed.astype(BF16)).reshape(group_rows, columns)
        branch = group_scatter(matmul(mixed_low, weight_out), rows)
        r_a = inverse_rms(branch)
        hidden_in = tokens.astype(F32) + branch * r_a * gain_a
        group_hidden_in = group_gather(hidden_in.astype(BF16))
        gate = matmul(group_hidden_in, weight_gate)
        up = matmul(group_hidden_in, weight_up)
        sig = 1.0 / (1.0 + jnp.exp(-gate))
        hidden = (gate * sig * up).astype(BF16)
        result = group_scatter(matmul(hidden, weight_down), rows)
        r_m = inverse_rms(result)
        out_tokens = (hidden_in + result * r_m * gain_f).astype(BF16)

        def norm_back(values, r, gain, grad):
            scaled = gain * grad
            mean = jnp.mean(scaled * values, -1, keepdims=True)
            return r * (scaled - values * (r * r) * mean), jnp.sum(grad * values * r, 0)

        grad_out = cotangent.astype(F32)
        result_grad, feed_gain_term = norm_back(result, r_m, gain_f, grad_out)
        group_result_grad = group_gather(result_grad.astype(BF16))

        def scatter(term):
            return lax.psum_scatter(term.astype(BF16), "r", scatter_dimension=0, tiled=True)

        g_w_down = scatter(inner_t(hidden, group_result_grad)).astype(F32)
        hidden_grad = matmul_t(group_result_grad, weight_down)
        gate_grad = (hidden_grad * up * sig * (1.0 + gate * (1.0 - sig))).astype(BF16)
        up_grad = (hidden_grad * gate * sig).astype(BF16)
        hidden_in_grad = cotangent.astype(F32) + group_scatter(
            matmul_t(gate_grad, weight_gate) + matmul_t(up_grad, weight_up), rows
        )
        gate_share = scatter(inner_t(group_hidden_in, gate_grad))
        up_share = scatter(inner_t(group_hidden_in, up_grad))
        branch_grad, mixer_gain_term = norm_back(branch, r_a, gain_a, hidden_in_grad)
        group_branch_grad = group_gather(branch_grad.astype(BF16))
        out_term = inner_t(mixed_low, group_branch_grad)
        mixed_grad = heads_of(matmul_t(group_branch_grad, weight_out).astype(BF16))
        softmax_grad = jnp.einsum("bqhd,bkhd->bhqk", mixed_grad, v, preferred_element_type=F32)
        inner = jnp.sum(softmax * softmax_grad, axis=-1, keepdims=True)
        score_grad = (softmax * (softmax_grad - inner)).astype(BF16)
        v_grad = jnp.einsum("bhqk,bqhd->bkhd", softmax_low, mixed_grad, preferred_element_type=F32)
        q_grad = jnp.einsum("bhqk,bkhd->bqhd", score_grad, k, preferred_element_type=F32) * scale
        k_grad = jnp.einsum("bhqk,bqhd->bkhd", score_grad, q, preferred_element_type=F32) * scale

        def flat(array):
            return from_block(array).reshape(group_rows, columns)

        q_back = turned(flat(q_grad), -sine)
        k_back = turned(flat(k_grad), -sine)
        means = jnp.stack([jnp.sum(q_back * gain_q * query, -1), jnp.sum(k_back * gain_k * key, -1)])
        mean_q, mean_k = (group_sum(means) / width)[:, :, None]
        query_grad = (r_q * (gain_q * q_back - query * (r_q * r_q) * mean_q)).astype(BF16)
        key_grad = (r_k * (gain_k * k_back - key * (r_k * r_k) * mean_k)).astype(BF16)
        query_gain_term = jnp.sum(q_back * query * r_q, 0)
        key_gain_term = jnp.sum(k_back * key * r_k, 0)
        grads = jnp.concatenate([query_grad, key_grad, flat(v_grad).astype(BF16)], 1)
        g_tokens = hidden_in_grad + group_scatter(matmul_t(grads, weight_qkv), rows)

        def from_units(share):
            parts = exchange(share.reshape(8, weight_rows, units))
            shaped = parts.reshape(8, weight_rows, replicas, unit_rows).transpose(1, 2, 0, 3)
            return shaped.reshape(weight_rows, 8 * units).astype(F32)

        qkv_share = scatter(inner_t(group_tokens, grads))
        qkv_parts = exchange(qkv_share.reshape(8, weight_rows, 3 * columns))
        qkv_parts = qkv_parts.reshape(head_groups, per_head, weight_rows, 3, own_heads, HEAD)
        g_qkv = qkv_parts.transpose(3, 2, 1, 4, 0, 5).reshape(3, weight_rows, width).astype(F32)
        out_parts = out_term.astype(BF16).reshape(own_heads, per_head, weight_rows, width).transpose(1, 0, 2, 3)
        out_parts = lax.all_to_all(out_parts, head_axes, 0, 0, tiled=True)
        g_w_out = scatter(out_parts.reshape(replicas * weight_rows, width)).astype(F32)
        g_w_gate = from_units(gate_share)
        g_w_up = from_units(up_share)

        head_terms = jnp.stack([query_gain_term, key_gain_term]).reshape(2, 1, own_heads, 1, HEAD)
        spread = jnp.zeros((2, per_head, own_heads, head_groups, HEAD), F32)
        spread = lax.dynamic_update_slice(spread, head_terms, (0, place, 0, head_group, 0))
        gain_terms = jnp.concatenate(
            [spread.reshape(2, width), jnp.stack([mixer_gain_term, feed_gain_term])], 0
        )
        g_gains = lax.psum_scatter(gain_terms, ALL, scatter_dimension=1, tiled=True)
        return (
            out_tokens,
            g_tokens,
            g_qkv[0],
            g_qkv[1],
            g_qkv[2],
            g_w_out,
            g_gains[0],
            g_gains[1],
            g_gains[2],
            g_w_gate,
            g_w_up,
            g_w_down,
            g_gains[3],
        )

    return body


def solution(mesh):
    count = mesh.shape["dev"]
    grid = Mesh(mesh.devices.reshape(count // 8, 2, 2, 2), ALL)

    def run(tokens, cotangent, segment_ids, piece_ids, w_query, *rest):
        per_head = count * HEAD // w_query.shape[0]
        rows, whole, gain = P(ALL, None), P(), P(ALL)
        in_specs = (rows, rows, whole, whole) + (rows,) * 4 + (gain,) * 3 + (rows,) * 3 + (gain,)
        out_specs = (rows,) * 6 + (gain,) * 3 + (rows,) * 3 + (gain,)
        return jax.shard_map(
            make_body((count // 8, per_head)), mesh=grid, in_specs=in_specs, out_specs=out_specs, check_vma=False
        )(tokens, cotangent, segment_ids, piece_ids, w_query, *rest)

    return run
```

```python
import math

import jax
import jax.numpy as jnp
from jax import lax
from jax.experimental import pallas as pl
from jax.experimental.pallas import tpu as pltpu
from jax.sharding import Mesh, PartitionSpec as P

HEAD = 128
SEQ_MAX = 1024
NORM_EPS = 1e-06
ROPE_BASE = 500000.0
MASKED = -1e30
BF16 = jnp.bfloat16
F32 = jnp.float32
GROUP = ("y", "x", "c")
ALL = ("zh", "zl", "y", "x", "c")
PLANES = ("zh", "zl")


def matmul(left, right):
    return jnp.dot(left, right, preferred_element_type=F32)


def matmul_t(left, right):
    return lax.dot_general(left, right, (((1,), (1,)), ((), ())), preferred_element_type=F32)


def inner_t(left, right):
    return lax.dot_general(left, right, (((0,), (0,)), ((), ())), preferred_element_type=F32)


def inverse_rms(values):
    return lax.rsqrt(jnp.mean(values * values, axis=-1, keepdims=True) + NORM_EPS)


def after(value, *others):
    return lax.optimization_barrier((value,) + others)[0]


def swap(block, axis):
    return lax.ppermute(block, axis, [(0, 1), (1, 0)])


def group_gather(own):
    half = own.shape[0] // 2
    near_x = swap(own, "x")
    near_y = swap(own, "y")
    top = swap(near_x[:half], "y")
    low = swap(near_y[half:], "x")
    first = jnp.concatenate([own, near_x, near_y], 0)
    last = jnp.concatenate([top, low], 0)
    return jnp.concatenate([first, last, swap(first, "c"), swap(last, "c")], 0)


def group_sum(terms):
    total = terms.reshape(terms.shape[0], 2, 2, 2, -1)
    for dim, axis in enumerate(("c", "y", "x")):
        total = total + jnp.flip(swap(total, axis), dim + 1)
    return total.reshape(terms.shape)


def group_scatter(parts, rows):
    width = parts.shape[1]
    half = rows // 2
    arrived = swap(parts[4 * rows :], "c")
    mine = parts[: 4 * rows].astype(F32) + arrived.astype(F32)
    mine = mine.astype(BF16).reshape(2, 2, 2, half, width)
    got_x = swap(mine[:, 1, 0], "x")
    got_y = swap(mine[1, :, 1], "y")
    top = mine[:, 0, 0].astype(F32) + got_x.astype(F32)
    bottom = mine[0, :, 1].astype(F32) + got_y.astype(F32)
    top_last = swap(top[1].astype(BF16), "y")
    bottom_last = swap(bottom[1].astype(BF16), "x")
    return jnp.concatenate([top[0] + top_last.astype(F32), bottom[0] + bottom_last.astype(F32)], 0)


def doubled(own, axes):
    for axis in reversed(axes):
        size = lax.axis_size(axis)
        step = 1
        while step < size:
            got = lax.ppermute(own, axis, [(i, i ^ step) for i in range(size)])
            low_side = lax.axis_index(axis) & step == 0
            own = jnp.concatenate([jnp.where(low_side, own, got), jnp.where(low_side, got, own)], 0)
            step *= 2
    return own


def halved(terms, axes):
    for axis in axes:
        size = lax.axis_size(axis)
        step = size // 2
        while step:
            low_side = lax.axis_index(axis) & step == 0
            first, second = jnp.split(terms, 2)
            got = lax.ppermute(
                jnp.where(low_side, second, first), axis, [(i, i ^ step) for i in range(size)]
            )
            terms = jnp.where(low_side, first, second) + got
            step //= 2
    return terms


def gather_planes(part):
    return lax.all_gather(part, PLANES, axis=0, tiled=True)


def scatter_planes(term):
    return lax.psum_scatter(term, PLANES, scatter_dimension=0, tiled=True)


SCALE = HEAD ** (-0.5)
ROWS = 256
PARAMS = pltpu.CompilerParams(vmem_limit_bytes=48 * 2**20)


def flat_rows(ref):
    return ref[...].reshape(-1, ref.shape[-1])


def turn(values, cosine, sine):
    return values * cosine + pltpu.roll(values, HEAD // 2, 1) * sine


def softmax_rows(query, key, place, info):
    scores = matmul_t(query, key) * SCALE
    visible = (place >= info[:, 0:1]) & (place < info[:, 1:2])
    masked = jnp.where(visible, scores, MASKED)
    weights = jnp.exp(masked - jnp.max(masked, -1, keepdims=True))
    return weights * (1.0 / jnp.sum(weights, -1, keepdims=True))


def attend_kernel(q_ref, k_ref, v_ref, info_ref, cos_ref, sin_ref, gq_ref, gk_ref, place_ref, o_ref):
    info, cosine, sine = flat_rows(info_ref), flat_rows(cos_ref), flat_rows(sin_ref)
    query = turn(flat_rows(q_ref) * info[:, 2:3] * gq_ref[...], cosine, sine).astype(BF16)
    key = turn(flat_rows(k_ref) * info[:, 3:4] * gk_ref[...], cosine, sine).astype(BF16)
    value = flat_rows(v_ref).astype(BF16)
    place = place_ref[...]
    for start in range(0, SEQ_MAX, ROWS):
        softmax = softmax_rows(query[start : start + ROWS], key, place, info[start : start + ROWS])
        mixed = matmul(softmax.astype(BF16), value).astype(BF16)
        half, at = divmod(start, SEQ_MAX // 2)
        o_ref[half, 0, at : at + ROWS] = mixed


def attend_back_kernel(
    q_ref, k_ref, v_ref, info_ref, cos_ref, sin_ref, gq_ref, gk_ref, place_ref, do_ref,
    dq_ref, dk_ref, dv_ref, mean_ref, dk_sum, dv_sum, dq_all,
):
    info, cosine, sine = flat_rows(info_ref), flat_rows(cos_ref), flat_rows(sin_ref)
    query_in, key_in = flat_rows(q_ref), flat_rows(k_ref)
    query = turn(query_in * info[:, 2:3] * gq_ref[...], cosine, sine).astype(BF16)
    key = turn(key_in * info[:, 3:4] * gk_ref[...], cosine, sine).astype(BF16)
    value = flat_rows(v_ref).astype(BF16)
    grad = flat_rows(do_ref)
    place = place_ref[...]
    for start in range(0, SEQ_MAX, ROWS):
        part = slice(start, start + ROWS)
        softmax = softmax_rows(query[part], key, place, info[part])
        softmax_grad = matmul_t(grad[part], value)
        inner = jnp.sum(softmax * softmax_grad, -1, keepdims=True)
        score_grad = (softmax * (softmax_grad - inner)).astype(BF16)
        dq_all[part] = matmul(score_grad, key) * SCALE
        dk_term = inner_t(score_grad, query[part])
        dv_term = inner_t(softmax.astype(BF16), grad[part])
        if start:
            dk_sum[...] += dk_term
            dv_sum[...] += dv_term
        else:
            dk_sum[...] = dk_term
            dv_sum[...] = dv_term
    dq = turn(dq_all[...], cosine, -sine)
    dk = turn(dk_sum[...] * SCALE, cosine, -sine)
    dq_ref[...] = dq.reshape(dq_ref.shape)
    dk_ref[...] = dk.reshape(dk_ref.shape)
    dv_ref[...] = dv_sum[...].astype(BF16).reshape(dv_ref.shape)
    mean_q = jnp.sum(dq * gq_ref[...] * query_in, -1, keepdims=True)
    mean_k = jnp.sum(dk * gk_ref[...] * key_in, -1, keepdims=True)
    mean_ref[...] = jnp.concatenate([mean_q, mean_k], 1).reshape(mean_ref.shape)


def qkv_grad_kernel(p_ref, dq_ref, dk_ref, dv_ref, info_ref, mean_ref, gq_ref, gk_ref, grads_ref, gains_ref):
    columns = dq_ref.shape[1]
    info, mean = info_ref[...], mean_ref[...]
    terms = []
    for i, (d_ref, gain_ref) in enumerate(((dq_ref, gq_ref), (dk_ref, gk_ref))):
        values, r, d = p_ref[:, i * columns : (i + 1) * columns], info[:, 2 + i : 3 + i], d_ref[...]
        grad = r * (gain_ref[...] * d - values * (r * r) * mean[:, i : i + 1])
        grads_ref[:, i * columns : (i + 1) * columns] = grad.astype(BF16)
        terms.append(jnp.sum(d * values * r, 0, keepdims=True))
    grads_ref[:, 2 * columns :] = dv_ref[...]
    term = jnp.concatenate(terms, 0)

    @pl.when(pl.program_id(0) == 0)
    def _():
        gains_ref[...] = term

    @pl.when(pl.program_id(0) > 0)
    def _():
        gains_ref[...] += term


def to_units(gate, up, unit_rows):
    rows, width = gate.shape
    units = width // 8

    def kernel(gate_ref, up_ref, out_ref):
        for i, w_ref in enumerate((gate_ref, up_ref)):
            for m in range(8):
                for r in range(units // unit_rows):
                    source, target = (r * 8 + m) * unit_rows, i * units + r * unit_rows
                    out_ref[m, :, target : target + unit_rows] = w_ref[:, source : source + unit_rows].astype(BF16)

    step = min(rows, 16)
    return pl.pallas_call(
        kernel,
        grid=(rows // step,),
        in_specs=[pl.BlockSpec((step, width), lambda i: (i, 0))] * 2,
        out_specs=pl.BlockSpec((8, step, 2 * units), lambda i: (0, i, 0)),
        out_shape=jax.ShapeDtypeStruct((8, rows, 2 * units), BF16),
        compiler_params=PARAMS,
    )(gate, up)


def from_units(parts, unit_rows):
    _, rows, units = parts.shape

    def kernel(p_ref, out_ref):
        for m in range(8):
            for r in range(units // unit_rows):
                target, source = (r * 8 + m) * unit_rows, r * unit_rows
                out_ref[:, target : target + unit_rows] = p_ref[m, :, source : source + unit_rows].astype(F32)

    step = min(rows, 16)
    return pl.pallas_call(
        kernel,
        grid=(rows // step,),
        in_specs=[pl.BlockSpec((8, step, units), lambda i: (0, i, 0))],
        out_specs=pl.BlockSpec((step, 8 * units), lambda i: (i, 0)),
        out_shape=jax.ShapeDtypeStruct((rows, 8 * units), F32),
        compiler_params=PARAMS,
    )(parts)


def head_specs(heads):
    def of(width, column):
        return pl.BlockSpec((2, 1, SEQ_MAX // 2, width), lambda b, h: (0, b, 0, column(h)))

    gain = pl.BlockSpec((1, HEAD), lambda b, h: (0, h))
    return of, [
        of(HEAD, lambda h: h),
        of(HEAD, lambda h: heads + h),
        of(HEAD, lambda h: 2 * heads + h),
        of(4, lambda h: 0),
        of(HEAD, lambda h: 0),
        of(HEAD, lambda h: 0),
        gain,
        gain,
        pl.BlockSpec((1, SEQ_MAX), lambda b, h: (0, 0)),
    ]


def in_blocks(array):
    return array.reshape(2, -1, SEQ_MAX // 2, array.shape[-1])


def attend(projected, info, cosine, sine, gain_q, gain_k, place):
    rows, columns = projected.shape[0], projected.shape[1] // 3
    heads, blocks = columns // HEAD, rows // SEQ_MAX
    of, specs = head_specs(heads)
    p = in_blocks(projected)
    mixed = pl.pallas_call(
        attend_kernel,
        grid=(blocks, heads),
        in_specs=specs,
        out_specs=of(HEAD, lambda h: h),
        out_shape=jax.ShapeDtypeStruct((2, blocks, SEQ_MAX // 2, columns), BF16),
        compiler_params=PARAMS,
        cost_estimate=pl.CostEstimate(
            flops=4 * rows * SEQ_MAX * columns, bytes_accessed=8 * rows * columns * 2, transcendentals=rows * SEQ_MAX * heads
        ),
    )(p, p, p, in_blocks(info), in_blocks(cosine), in_blocks(sine), gain_q, gain_k, place)
    return mixed.reshape(rows, columns)


def attend_back(projected, info, cosine, sine, gain_q, gain_k, place, mixed_grad):
    rows, columns = projected.shape[0], projected.shape[1] // 3
    heads, blocks = columns // HEAD, rows // SEQ_MAX
    of, specs = head_specs(heads)
    p = in_blocks(projected)
    shape = (2, blocks, SEQ_MAX // 2, columns)
    dq, dk, dv, means = pl.pallas_call(
        attend_back_kernel,
        grid=(blocks, heads),
        in_specs=specs + [of(HEAD, lambda h: h)],
        out_specs=[of(HEAD, lambda h: h)] * 3
        + [pl.BlockSpec((1, 2, 1, SEQ_MAX // 2, 2), lambda b, h: (h, 0, b, 0, 0))],
        out_shape=[
            jax.ShapeDtypeStruct(shape, F32),
            jax.ShapeDtypeStruct(shape, F32),
            jax.ShapeDtypeStruct(shape, BF16),
            jax.ShapeDtypeStruct((heads,) + shape[:3] + (2,), F32),
        ],
        scratch_shapes=[pltpu.VMEM((SEQ_MAX, HEAD), F32)] * 3,
        compiler_params=PARAMS,
        cost_estimate=pl.CostEstimate(
            flops=10 * rows * SEQ_MAX * columns, bytes_accessed=12 * rows * columns * 2, transcendentals=rows * SEQ_MAX * heads
        ),
    )(p, p, p, in_blocks(info), in_blocks(cosine), in_blocks(sine), gain_q, gain_k, place, in_blocks(mixed_grad))
    flat = [array.reshape(rows, columns) for array in (dq, dk, dv)]
    return *flat, jnp.sum(means, 0).reshape(rows, 2)


def qkv_grads(projected, dq, dk, dv, info, mean, gain_q, gain_k):
    rows, columns = dq.shape
    step = 512

    def by_row(width):
        return pl.BlockSpec((step, width), lambda i: (i, 0))

    def fixed(height):
        return pl.BlockSpec((height, columns), lambda i: (0, 0))

    return pl.pallas_call(
        qkv_grad_kernel,
        grid=(rows // step,),
        in_specs=[by_row(3 * columns)] + [by_row(columns)] * 3 + [by_row(4), by_row(2), fixed(1), fixed(1)],
        out_specs=[by_row(3 * columns), fixed(2)],
        out_shape=[
            jax.ShapeDtypeStruct((rows, 3 * columns), BF16),
            jax.ShapeDtypeStruct((2, columns), F32),
        ],
        compiler_params=PARAMS,
    )(projected, dq, dk, dv, info, mean, gain_q, gain_k)


def make_body(count, per_head):
    replicas = count // 8
    own_heads = replicas // per_head
    head_axes = GROUP[3 - int(math.log2(per_head)) :]
    head_shape = (per_head, own_heads, 8 // per_head)
    head_shape_put = (8 // per_head, per_head, own_heads)

    def body(
        tokens,
        cotangent,
        segment_ids,
        piece_ids,
        w_query,
        w_key,
        w_value,
        w_out,
        query_gain,
        key_gain,
        mixer_gain,
        w_gate,
        w_up,
        w_down,
        feed_gain,
    ):
        rows, width = tokens.shape
        weight_rows = w_query.shape[0]
        unit_rows = w_down.shape[0]
        units = replicas * unit_rows
        columns = own_heads * HEAD
        group_rows = 8 * rows
        blocks = group_rows // SEQ_MAX
        member = lax.axis_index(GROUP)
        device = lax.axis_index(ALL)

        def by_head(weight):
            shaped = weight.astype(BF16).reshape((weight_rows,) + head_shape + (HEAD,))
            return shaped.transpose(3, 1, 0, 2, 4).reshape(8, weight_rows, columns)

        def exchange(parts, group):
            return lax.all_to_all(parts, group, 0, 0, tiled=True)

        own_gains = jnp.stack([query_gain, key_gain, mixer_gain, feed_gain]).astype(BF16)
        plane_gains = doubled(own_gains.reshape(1, 4, weight_rows), PLANES)
        gains = doubled(plane_gains, GROUP).reshape(8, replicas, 4, weight_rows)
        gains = gains.transpose(2, 1, 0, 3).reshape(4, width).astype(F32)

        qkv_parts = jnp.concatenate([by_head(w_query), by_head(w_key), by_head(w_value)], 2)
        qkv_piece = exchange(qkv_parts, GROUP).reshape(8 * weight_rows, 3 * columns)
        out_halves = gather_planes(after(w_out.astype(BF16), plane_gains))
        feed_parts = after(to_units(w_gate, w_up, unit_rows), qkv_piece)
        feed_piece = exchange(feed_parts, GROUP).reshape(8 * weight_rows, 2 * units)
        group_tokens = group_gather(after(tokens, qkv_piece))
        weight_qkv = gather_planes(after(qkv_piece, plane_gains))
        weight_feed = gather_planes(feed_piece)
        weight_down = gather_planes(after(w_down.astype(BF16), weight_qkv))
        out_halves = out_halves.reshape(per_head, own_heads, weight_rows, width)
        out_heads = lax.all_to_all(out_halves, head_axes, 0, 0, tiled=True)
        weight_out = out_heads.transpose(1, 0, 2, 3).reshape(columns, width)

        head_gains = gains[:2].reshape((2,) + head_shape + (HEAD,)).transpose(0, 3, 1, 2, 4)
        head_gains = lax.dynamic_index_in_dim(head_gains.reshape(2, 8, columns), member, 1, keepdims=False)
        gain_q, gain_k = head_gains.reshape(2, 1, columns)
        gain_a, gain_f = gains[2:3], gains[3:4]

        orders = [c + 4 * y + 2 * x for c in (0, 1) for y in (0, 1) for x in (0, 1)]
        starts = [(device ^ k) * rows for k in orders]

        def of_group(ids):
            return jnp.concatenate([lax.dynamic_slice_in_dim(ids, s, rows, 0) for s in starts])

        places = jnp.concatenate([s + jnp.arange(rows, dtype=jnp.int32) for s in starts])

        def by_block(array):
            shaped = array.reshape((2, blocks, group_rows // (2 * blocks)) + array.shape[1:])
            return jnp.moveaxis(shaped, 1, 0).reshape((blocks, SEQ_MAX) + array.shape[1:])

        def from_block(array):
            shaped = array.reshape((blocks, 2, SEQ_MAX // 2) + array.shape[2:])
            return jnp.moveaxis(shaped, 0, 1).reshape((group_rows,) + array.shape[2:])

        segment = by_block(of_group(segment_ids))
        piece = by_block(of_group(piece_ids))
        place_block = by_block(places) % SEQ_MAX
        before = jnp.sum((segment[:, None, :] < segment[:, :, None]).astype(jnp.int32), -1)
        positions = from_block(place_block - before)
        in_piece = (piece[:, None, :] == piece[:, :, None]) & (piece[:, :, None] > 0)
        piece_end = jnp.max(jnp.where(in_piece, place_block[:, None, :] + 1, 0), -1)
        first_seen = from_block(before).astype(F32)
        end_seen = from_block(jnp.maximum(place_block + 1, piece_end)).astype(F32)
        place = place_block[:1].astype(F32)
        freqs = jnp.exp(jnp.arange(HEAD // 2, dtype=F32) * (-2.0 * math.log(ROPE_BASE) / HEAD))
        angles = positions.astype(F32)[:, None] * freqs[None, :]
        cosine = jnp.concatenate([jnp.cos(angles), jnp.cos(angles)], 1)
        sine = jnp.concatenate([-jnp.sin(angles), jnp.sin(angles)], 1)

        projected = matmul(after(group_tokens, feed_piece), weight_qkv)
        squares = jnp.sum(jnp.square(projected[:, : 2 * columns]).reshape(group_rows, 2, columns), -1)
        inverse = lax.rsqrt(group_sum(squares.T) / width + NORM_EPS)
        inverse = after(inverse, weight_out)
        info = jnp.stack([first_seen, end_seen, inverse[0], inverse[1]], 1)
        attention = (projected, info, cosine, sine, gain_q, gain_k, place)
        mixed_low = attend(*attention)
        branch = group_scatter(matmul(mixed_low, weight_out).astype(BF16), rows)
        r_a = inverse_rms(branch)
        hidden_in = tokens.astype(F32) + branch * r_a * gain_a
        group_hidden_in = group_gather(hidden_in.astype(BF16))
        gate = matmul(group_hidden_in, weight_feed[:, :units])
        up = matmul(group_hidden_in, weight_feed[:, units:])
        sig = 1.0 / (1.0 + jnp.exp(-gate))
        hidden = (gate * sig * up).astype(BF16)
        result = group_scatter(matmul(hidden, weight_down).astype(BF16), rows)
        r_m = inverse_rms(result)
        out_tokens = (hidden_in + result * r_m * gain_f).astype(BF16)

        def norm_back(values, r, gain, grad):
            scaled = gain * grad
            mean = jnp.mean(scaled * values, -1, keepdims=True)
            return r * (scaled - values * (r * r) * mean), jnp.sum(grad * values * r, 0)

        grad_out = cotangent.astype(F32)
        result_grad, feed_gain_term = norm_back(result, r_m, gain_f, grad_out)
        group_result_grad = group_gather(result_grad.astype(BF16))

        down_term = inner_t(hidden, group_result_grad).astype(BF16)
        hidden_grad = matmul_t(after(group_result_grad, down_term), weight_down)
        gate_grad = (hidden_grad * up * sig * (1.0 + gate * (1.0 - sig))).astype(BF16)
        up_grad = (hidden_grad * gate * sig).astype(BF16)
        hidden_in_parts = (
            matmul_t(gate_grad, weight_feed[:, :units]) + matmul_t(up_grad, weight_feed[:, units:])
        ).astype(BF16)
        gate_term = inner_t(after(group_hidden_in, hidden_in_parts), gate_grad).astype(BF16)
        up_term = inner_t(after(group_hidden_in, gate_term), up_grad).astype(BF16)
        down_share = scatter_planes(down_term)
        gate_share = scatter_planes(gate_term)
        up_share = scatter_planes(up_term)
        hidden_in_grad = grad_out + group_scatter(hidden_in_parts, rows)
        hidden_in_grad = after(hidden_in_grad, up_term)
        branch_grad, mixer_gain_term = norm_back(branch, r_a, gain_a, hidden_in_grad)
        group_branch_grad = group_gather(branch_grad.astype(BF16))
        group_branch_grad = after(group_branch_grad, down_share)
        mixed_grad = matmul_t(group_branch_grad, weight_out).astype(BF16)
        q_back, k_back, v_grad, means = attend_back(*attention, mixed_grad)
        out_term = inner_t(mixed_low, after(group_branch_grad, mixed_grad))
        means = after(means, gate_share, out_term)
        means = group_sum(means.T).T / width
        grads, head_terms = qkv_grads(projected, q_back, k_back, v_grad, info, means, gain_q, gain_k)
        qkv_term = inner_t(group_tokens, grads).astype(BF16)
        grads = after(grads, qkv_term)
        g_tokens = hidden_in_grad + group_scatter(matmul_t(grads, weight_qkv).astype(BF16), rows)

        qkv_share = scatter_planes(qkv_term)
        qkv_back = exchange(qkv_share.reshape(8, weight_rows, 3 * columns), GROUP)
        qkv_back = qkv_back.reshape(head_shape_put[:2] + (weight_rows, 3, own_heads, HEAD))
        g_qkv = qkv_back.transpose(3, 2, 1, 4, 0, 5).reshape(3, weight_rows, width).astype(F32)
        out_parts = out_term.astype(BF16).reshape(own_heads, per_head, weight_rows, width)
        out_parts = lax.all_to_all(out_parts.transpose(1, 0, 2, 3), head_axes, 0, 0, tiled=True)
        g_w_out = scatter_planes(out_parts.reshape(replicas * weight_rows, width)).astype(F32)
        g_w_down = down_share.astype(F32)
        g_w_gate = from_units(exchange(gate_share.reshape(8, weight_rows, units), GROUP), unit_rows)
        g_w_up = from_units(exchange(up_share.reshape(8, weight_rows, units), GROUP), unit_rows)

        head_terms = head_terms.reshape(2, 1, columns)
        spread = jnp.zeros((2, 8, columns), F32)
        spread = lax.dynamic_update_slice(spread, head_terms, (0, member, 0))
        spread = spread.reshape((2,) + head_shape_put + (HEAD,)).transpose(0, 2, 3, 1, 4)
        gain_terms = jnp.concatenate([spread.reshape(2, width), jnp.stack([mixer_gain_term, feed_gain_term])], 0)
        gain_terms = gain_terms.reshape(4, replicas, 8, weight_rows).transpose(2, 1, 0, 3)
        g_gains = halved(gain_terms.reshape(count, 4, weight_rows), GROUP + PLANES)[0]
        return (
            out_tokens,
            g_tokens,
            g_qkv[0],
            g_qkv[1],
            g_qkv[2],
            g_w_out,
            g_gains[0],
            g_gains[1],
            g_gains[2],
            g_w_gate,
            g_w_up,
            g_w_down,
            g_gains[3],
        )

    return body


def solution(mesh):
    count = mesh.shape["dev"]
    grid = Mesh(mesh.devices.reshape(count // 16, 2, 2, 2, 2), ALL)

    def run(tokens, cotangent, segment_ids, piece_ids, w_query, *rest):
        per_head = count * HEAD // w_query.shape[0]
        rows, whole, gain = P(ALL, None), P(), P(ALL)
        in_specs = (rows, rows, whole, whole) + (rows,) * 4 + (gain,) * 3 + (rows,) * 3 + (gain,)
        out_specs = (rows,) * 6 + (gain,) * 3 + (rows,) * 3 + (gain,)
        return jax.shard_map(
            make_body(count, per_head), mesh=grid, in_specs=in_specs, out_specs=out_specs, check_vma=False
        )(tokens, cotangent, segment_ids, piece_ids, w_query, *rest)

    return run
```

```python
import math

import jax
import jax.numpy as jnp
from jax import lax
from jax.experimental import pallas as pl
from jax.experimental.pallas import tpu as pltpu
from jax.sharding import Mesh, PartitionSpec as P

HEAD = 128
SEQ_MAX = 1024
NORM_EPS = 1e-06
ROPE_BASE = 500000.0
MASKED = -1e30
BF16 = jnp.bfloat16
F32 = jnp.float32
GROUP = ("y", "x", "c")
ALL = ("zh", "zl", "y", "x", "c")
PLANES = ("zh", "zl")


def matmul(left, right):
    return jnp.dot(left, right, preferred_element_type=F32)


def matmul_t(left, right):
    return lax.dot_general(left, right, (((1,), (1,)), ((), ())), preferred_element_type=F32)


def inner_t(left, right):
    return lax.dot_general(left, right, (((0,), (0,)), ((), ())), preferred_element_type=F32)


def inverse_rms(values):
    return lax.rsqrt(jnp.mean(values * values, axis=-1, keepdims=True) + NORM_EPS)


def after(value, *others):
    return lax.optimization_barrier((value,) + others)[0]


def region(function, ids, *operands):
    def nothing(*operands):
        return jax.tree.map(lambda leaf: jnp.zeros(leaf.shape, leaf.dtype), jax.eval_shape(function, *operands))

    return lax.cond(ids[0] == 0, function, nothing, *operands)


def swap(block, axis):
    return lax.ppermute(block, axis, [(0, 1), (1, 0)])


def group_gather(own):
    half = own.shape[0] // 2
    near_x = swap(own, "x")
    near_y = swap(own, "y")
    top = swap(near_x[:half], "y")
    low = swap(near_y[half:], "x")
    first = jnp.concatenate([own, near_x, near_y], 0)
    last = jnp.concatenate([top, low], 0)
    return jnp.concatenate([first, last, swap(first, "c"), swap(last, "c")], 0)


def group_sum(terms):
    total = terms.reshape(terms.shape[0], 2, 2, 2, -1)
    for dim, axis in enumerate(("c", "y", "x")):
        total = total + jnp.flip(swap(total, axis), dim + 1)
    return total.reshape(terms.shape)


def scatter_start(parts, rows, *others):
    width = parts.shape[1]
    half = rows // 2
    arrived = swap(parts[4 * rows :], "c")
    mine = parts[: 4 * rows].astype(F32) + arrived.astype(F32)
    mine = mine.astype(BF16).reshape(2, 2, 2, half, width)
    got_x = after(swap(mine[:, 1, 0], "x"), *others)
    got_y = after(swap(mine[1, :, 1], "y"), *others)
    return mine[:, 0, 0].astype(F32) + got_x.astype(F32), mine[0, :, 1].astype(F32) + got_y.astype(F32)


def scatter_end(top, bottom):
    top_last = swap(top[1].astype(BF16), "y")
    bottom_last = swap(bottom[1].astype(BF16), "x")
    return jnp.concatenate([top[0] + top_last.astype(F32), bottom[0] + bottom_last.astype(F32)], 0)


def group_scatter(parts, rows):
    return scatter_end(*scatter_start(parts, rows))


def doubled(own, axes):
    for axis in reversed(axes):
        size = lax.axis_size(axis)
        step = 1
        while step < size:
            got = lax.ppermute(own, axis, [(i, i ^ step) for i in range(size)])
            low_side = lax.axis_index(axis) & step == 0
            own = jnp.concatenate([jnp.where(low_side, own, got), jnp.where(low_side, got, own)], 0)
            step *= 2
    return own


def halved(terms, axes):
    for axis in axes:
        size = lax.axis_size(axis)
        step = size // 2
        while step:
            low_side = lax.axis_index(axis) & step == 0
            first, second = jnp.split(terms, 2)
            got = lax.ppermute(
                jnp.where(low_side, second, first), axis, [(i, i ^ step) for i in range(size)]
            )
            terms = jnp.where(low_side, first, second) + got
            step //= 2
    return terms


def gather_planes(part):
    return lax.all_gather(part, PLANES, axis=0, tiled=True)


def scatter_planes(term):
    return lax.psum_scatter(term, PLANES, scatter_dimension=0, tiled=True)


SCALE = HEAD ** (-0.5)
ROWS = 256
PARAMS = pltpu.CompilerParams(vmem_limit_bytes=56 * 2**20)


def flat_rows(ref):
    return ref[...].reshape(-1, ref.shape[-1])


def turn(values, cosine, sine):
    return values * cosine + pltpu.roll(values, HEAD // 2, 1) * sine


def softmax_rows(query, key, place, info):
    scores = matmul_t(query, key) * SCALE
    visible = (place >= info[:, 0:1]) & (place < info[:, 1:2])
    masked = jnp.where(visible, scores, MASKED)
    weights = jnp.exp(masked - jnp.max(masked, -1, keepdims=True))
    return weights * (1.0 / jnp.sum(weights, -1, keepdims=True))


def attend_kernel(q_ref, k_ref, v_ref, info_ref, cos_ref, sin_ref, gq_ref, gk_ref, place_ref, o_ref):
    info, cosine, sine = flat_rows(info_ref), flat_rows(cos_ref), flat_rows(sin_ref)
    query = turn(flat_rows(q_ref) * info[:, 2:3] * gq_ref[...], cosine, sine).astype(BF16)
    key = turn(flat_rows(k_ref) * info[:, 3:4] * gk_ref[...], cosine, sine).astype(BF16)
    value = flat_rows(v_ref).astype(BF16)
    place = place_ref[...]
    for start in range(0, SEQ_MAX, ROWS):
        softmax = softmax_rows(query[start : start + ROWS], key, place, info[start : start + ROWS])
        mixed = matmul(softmax.astype(BF16), value).astype(BF16)
        half, at = divmod(start, SEQ_MAX // 2)
        o_ref[half, 0, at : at + ROWS] = mixed


def attend_back_kernel(
    q_ref, k_ref, v_ref, info_ref, cos_ref, sin_ref, gq_ref, gk_ref, place_ref, do_ref,
    dq_ref, dk_ref, dv_ref, mean_ref, dk_sum, dv_sum, dq_all,
):
    info, cosine, sine = flat_rows(info_ref), flat_rows(cos_ref), flat_rows(sin_ref)
    query_in, key_in = flat_rows(q_ref), flat_rows(k_ref)
    query = turn(query_in * info[:, 2:3] * gq_ref[...], cosine, sine).astype(BF16)
    key = turn(key_in * info[:, 3:4] * gk_ref[...], cosine, sine).astype(BF16)
    value = flat_rows(v_ref).astype(BF16)
    grad = flat_rows(do_ref)
    place = place_ref[...]
    for start in range(0, SEQ_MAX, ROWS):
        part = slice(start, start + ROWS)
        softmax = softmax_rows(query[part], key, place, info[part])
        softmax_grad = matmul_t(grad[part], value)
        inner = jnp.sum(softmax * softmax_grad, -1, keepdims=True)
        score_grad = (softmax * (softmax_grad - inner)).astype(BF16)
        dq_all[part] = matmul(score_grad, key) * SCALE
        dk_term = inner_t(query[part], score_grad)
        dv_term = inner_t(grad[part], softmax.astype(BF16))
        if start:
            dk_sum[...] += dk_term
            dv_sum[...] += dv_term
        else:
            dk_sum[...] = dk_term
            dv_sum[...] = dv_term
    dq = turn(dq_all[...], cosine, -sine)
    dk = turn(dk_sum[...].T * SCALE, cosine, -sine)
    dq_ref[...] = dq.reshape(dq_ref.shape)
    dk_ref[...] = dk.reshape(dk_ref.shape)
    dv_ref[...] = dv_sum[...].T.astype(BF16).reshape(dv_ref.shape)
    mean_q = jnp.sum(dq * gq_ref[...] * query_in, -1, keepdims=True)
    mean_k = jnp.sum(dk * gk_ref[...] * key_in, -1, keepdims=True)
    mean_ref[...] = jnp.concatenate([mean_q, mean_k], 1).reshape(mean_ref.shape)


def qkv_grad_kernel(p_ref, dq_ref, dk_ref, dv_ref, info_ref, mean_ref, gq_ref, gk_ref, grads_ref, gains_ref):
    columns = dq_ref.shape[1]
    info, mean = info_ref[...], mean_ref[...]
    terms = []
    for i, (d_ref, gain_ref) in enumerate(((dq_ref, gq_ref), (dk_ref, gk_ref))):
        values, r, d = p_ref[:, i * columns : (i + 1) * columns], info[:, 2 + i : 3 + i], d_ref[...]
        grad = r * (gain_ref[...] * d - values * (r * r) * mean[:, i : i + 1])
        grads_ref[:, i * columns : (i + 1) * columns] = grad.astype(BF16)
        terms.append(jnp.sum(d * values * r, 0, keepdims=True))
    grads_ref[:, 2 * columns :] = dv_ref[...]
    term = jnp.concatenate(terms, 0)

    @pl.when(pl.program_id(0) == 0)
    def _():
        gains_ref[...] = term

    @pl.when(pl.program_id(0) > 0)
    def _():
        gains_ref[...] += term


def to_units(gate, up, unit_rows):
    rows, width = gate.shape
    units = width // 8

    def kernel(gate_ref, up_ref, out_ref):
        for i, w_ref in enumerate((gate_ref, up_ref)):
            for m in range(8):
                for r in range(units // unit_rows):
                    source, target = (r * 8 + m) * unit_rows, i * units + r * unit_rows
                    out_ref[m, :, target : target + unit_rows] = w_ref[:, source : source + unit_rows].astype(BF16)

    step = min(rows, 16)
    return pl.pallas_call(
        kernel,
        grid=(rows // step,),
        in_specs=[pl.BlockSpec((step, width), lambda i: (i, 0))] * 2,
        out_specs=pl.BlockSpec((8, step, 2 * units), lambda i: (0, i, 0)),
        out_shape=jax.ShapeDtypeStruct((8, rows, 2 * units), BF16),
        compiler_params=PARAMS,
    )(gate, up)


def from_units(parts, unit_rows):
    _, rows, units = parts.shape
    units //= 2

    def kernel(p_ref, *out_refs):
        for i, out_ref in enumerate(out_refs):
            for m in range(8):
                for r in range(units // unit_rows):
                    target, source = (r * 8 + m) * unit_rows, i * units + r * unit_rows
                    out_ref[:, target : target + unit_rows] = p_ref[m, :, source : source + unit_rows].astype(F32)

    step = min(rows, 16)
    return pl.pallas_call(
        kernel,
        grid=(rows // step,),
        in_specs=[pl.BlockSpec((8, step, 2 * units), lambda i: (0, i, 0))],
        out_specs=[pl.BlockSpec((step, 8 * units), lambda i: (i, 0))] * 2,
        out_shape=[jax.ShapeDtypeStruct((rows, 8 * units), F32)] * 2,
        compiler_params=PARAMS,
    )(parts)


def from_heads(parts, members):
    _, rows, columns = parts.shape
    columns //= 3

    def kernel(p_ref, *out_refs):
        for i, out_ref in enumerate(out_refs):
            for m, targets in enumerate(members):
                for j, head in enumerate(targets):
                    source = i * columns + j * HEAD
                    out_ref[:, head * HEAD : (head + 1) * HEAD] = p_ref[m, :, source : source + HEAD].astype(F32)

    step = min(rows, 16)
    return pl.pallas_call(
        kernel,
        grid=(rows // step,),
        in_specs=[pl.BlockSpec((8, step, 3 * columns), lambda i: (0, i, 0))],
        out_specs=[pl.BlockSpec((step, 8 * columns), lambda i: (i, 0))] * 3,
        out_shape=[jax.ShapeDtypeStruct((rows, 8 * columns), F32)] * 3,
        compiler_params=PARAMS,
    )(parts)


def whole(array):
    return pl.BlockSpec(array.shape, lambda i: (0, 0), pipeline_mode=pl.Buffered(1))


def by_rows(step, width):
    return pl.BlockSpec((step, width), lambda i: (i, 0))


def gate_up(values, weight):
    rows, depth = values.shape
    units = weight.shape[1] // 2

    def kernel(v_ref, w_ref, both_ref, hidden_ref):
        for c in range(0, units, 512):
            gate = matmul(v_ref[...], w_ref[:, c : c + 512])
            up = matmul(v_ref[...], w_ref[:, units + c : units + c + 512])
            both_ref[:, c : c + 512] = gate
            both_ref[:, units + c : units + c + 512] = up
            hidden_ref[:, c : c + 512] = (gate / (1.0 + jnp.exp(-gate)) * up).astype(BF16)

    return pl.pallas_call(
        kernel,
        grid=(rows // ROWS,),
        in_specs=[by_rows(ROWS, depth), whole(weight)],
        out_specs=[by_rows(ROWS, 2 * units), by_rows(ROWS, units)],
        out_shape=[jax.ShapeDtypeStruct((rows, 2 * units), F32), jax.ShapeDtypeStruct((rows, units), BF16)],
        compiler_params=PARAMS,
        cost_estimate=pl.CostEstimate(
            flops=4 * rows * depth * units, bytes_accessed=14 * rows * units, transcendentals=rows * units
        ),
    )(values, weight)


def gate_up_back(grad, weight, both):
    rows, depth = grad.shape
    units = weight.shape[0]

    def kernel(g_ref, w_ref, both_ref, out_ref):
        for c in range(0, units, 512):
            hidden_grad = matmul_t(g_ref[...], w_ref[c : c + 512, :])
            gate, up = both_ref[:, c : c + 512], both_ref[:, units + c : units + c + 512]
            sig = 1.0 / (1.0 + jnp.exp(-gate))
            out_ref[:, c : c + 512] = (hidden_grad * up * sig * (1.0 + gate * (1.0 - sig))).astype(BF16)
            out_ref[:, units + c : units + c + 512] = (hidden_grad * (gate * sig)).astype(BF16)

    return pl.pallas_call(
        kernel,
        grid=(rows // ROWS,),
        in_specs=[by_rows(ROWS, depth), whole(weight), by_rows(ROWS, 2 * units)],
        out_specs=by_rows(ROWS, 2 * units),
        out_shape=jax.ShapeDtypeStruct((rows, 2 * units), BF16),
        compiler_params=PARAMS,
        cost_estimate=pl.CostEstimate(
            flops=2 * rows * depth * units, bytes_accessed=16 * rows * units, transcendentals=rows * units
        ),
    )(grad, weight, both)


def times_transposed(values, weight):
    rows, depth = values.shape
    width = weight.shape[0]

    def kernel(v_ref, w_ref, out_ref):
        for c in range(0, width, 512):
            out_ref[:, c : c + 512] = matmul_t(v_ref[...], w_ref[c : c + 512, :]).astype(BF16)

    return pl.pallas_call(
        kernel,
        grid=(rows // ROWS,),
        in_specs=[by_rows(ROWS, depth), whole(weight)],
        out_specs=by_rows(ROWS, width),
        out_shape=jax.ShapeDtypeStruct((rows, width), BF16),
        compiler_params=PARAMS,
        cost_estimate=pl.CostEstimate(
            flops=2 * rows * depth * width, bytes_accessed=2 * rows * (depth + width), transcendentals=0
        ),
    )(values, weight)


def head_specs(heads):
    def of(width, column):
        return pl.BlockSpec((2, 1, SEQ_MAX // 2, width), lambda b, h: (0, b, 0, column(h)))

    gain = pl.BlockSpec((1, HEAD), lambda b, h: (0, h))
    return of, [
        of(HEAD, lambda h: h),
        of(HEAD, lambda h: heads + h),
        of(HEAD, lambda h: 2 * heads + h),
        of(4, lambda h: 0),
        of(HEAD, lambda h: 0),
        of(HEAD, lambda h: 0),
        gain,
        gain,
        pl.BlockSpec((1, SEQ_MAX), lambda b, h: (0, 0)),
    ]


def in_blocks(array):
    return array.reshape(2, -1, SEQ_MAX // 2, array.shape[-1])


def attend(projected, info, cosine, sine, gain_q, gain_k, place):
    rows, columns = projected.shape[0], projected.shape[1] // 3
    heads, blocks = columns // HEAD, rows // SEQ_MAX
    of, specs = head_specs(heads)
    p = in_blocks(projected)
    mixed = pl.pallas_call(
        attend_kernel,
        grid=(blocks, heads),
        in_specs=specs,
        out_specs=of(HEAD, lambda h: h),
        out_shape=jax.ShapeDtypeStruct((2, blocks, SEQ_MAX // 2, columns), BF16),
        compiler_params=PARAMS,
        cost_estimate=pl.CostEstimate(
            flops=4 * rows * SEQ_MAX * columns, bytes_accessed=8 * rows * columns * 2, transcendentals=rows * SEQ_MAX * heads
        ),
    )(p, p, p, in_blocks(info), in_blocks(cosine), in_blocks(sine), gain_q, gain_k, place)
    return mixed.reshape(rows, columns)


def attend_back(projected, info, cosine, sine, gain_q, gain_k, place, mixed_grad):
    rows, columns = projected.shape[0], projected.shape[1] // 3
    heads, blocks = columns // HEAD, rows // SEQ_MAX
    of, specs = head_specs(heads)
    p = in_blocks(projected)
    shape = (2, blocks, SEQ_MAX // 2, columns)
    dq, dk, dv, means = pl.pallas_call(
        attend_back_kernel,
        grid=(blocks, heads),
        in_specs=specs + [of(HEAD, lambda h: h)],
        out_specs=[of(HEAD, lambda h: h)] * 3
        + [pl.BlockSpec((1, 2, 1, SEQ_MAX // 2, 2), lambda b, h: (h, 0, b, 0, 0))],
        out_shape=[
            jax.ShapeDtypeStruct(shape, F32),
            jax.ShapeDtypeStruct(shape, F32),
            jax.ShapeDtypeStruct(shape, BF16),
            jax.ShapeDtypeStruct((heads,) + shape[:3] + (2,), F32),
        ],
        scratch_shapes=[pltpu.VMEM((HEAD, SEQ_MAX), F32)] * 2 + [pltpu.VMEM((SEQ_MAX, HEAD), F32)],
        compiler_params=PARAMS,
        cost_estimate=pl.CostEstimate(
            flops=10 * rows * SEQ_MAX * columns, bytes_accessed=12 * rows * columns * 2, transcendentals=rows * SEQ_MAX * heads
        ),
    )(p, p, p, in_blocks(info), in_blocks(cosine), in_blocks(sine), gain_q, gain_k, place, in_blocks(mixed_grad))
    flat = [array.reshape(rows, columns) for array in (dq, dk, dv)]
    return *flat, jnp.sum(means, 0).reshape(rows, 2)


def qkv_grads(projected, dq, dk, dv, info, mean, gain_q, gain_k):
    rows, columns = dq.shape
    step = 512

    def by_row(width):
        return pl.BlockSpec((step, width), lambda i: (i, 0))

    def fixed(height):
        return pl.BlockSpec((height, columns), lambda i: (0, 0))

    return pl.pallas_call(
        qkv_grad_kernel,
        grid=(rows // step,),
        in_specs=[by_row(3 * columns)] + [by_row(columns)] * 3 + [by_row(4), by_row(2), fixed(1), fixed(1)],
        out_specs=[by_row(3 * columns), fixed(2)],
        out_shape=[
            jax.ShapeDtypeStruct((rows, 3 * columns), BF16),
            jax.ShapeDtypeStruct((2, columns), F32),
        ],
        compiler_params=PARAMS,
    )(projected, dq, dk, dv, info, mean, gain_q, gain_k)


def make_body(count, per_head):
    replicas = count // 8
    own_heads = replicas // per_head
    head_axes = GROUP[3 - int(math.log2(per_head)) :]
    head_shape = (per_head, own_heads, 8 // per_head)
    head_shape_put = (8 // per_head, per_head, own_heads)

    def body(
        tokens,
        cotangent,
        segment_ids,
        piece_ids,
        w_query,
        w_key,
        w_value,
        w_out,
        query_gain,
        key_gain,
        mixer_gain,
        w_gate,
        w_up,
        w_down,
        feed_gain,
    ):
        rows, width = tokens.shape
        weight_rows = w_query.shape[0]
        unit_rows = w_down.shape[0]
        units = replicas * unit_rows
        columns = own_heads * HEAD
        group_rows = 8 * rows
        blocks = group_rows // SEQ_MAX
        member = lax.axis_index(GROUP)
        device = lax.axis_index(ALL)

        def by_head(weight):
            shaped = weight.astype(BF16).reshape((weight_rows,) + head_shape + (HEAD,))
            return shaped.transpose(3, 1, 0, 2, 4).reshape(8, weight_rows, columns)

        def exchange(parts, group):
            return lax.all_to_all(parts, group, 0, 0, tiled=True)

        own_gains = jnp.stack([query_gain, key_gain, mixer_gain, feed_gain]).astype(BF16)
        plane_gains = doubled(own_gains.reshape(1, 4, weight_rows), PLANES)
        gains = doubled(plane_gains, GROUP).reshape(8, replicas, 4, weight_rows)
        gains = gains.transpose(2, 1, 0, 3).reshape(4, width).astype(F32)

        qkv_parts = jnp.concatenate([by_head(w_query), by_head(w_key), by_head(w_value)], 2)
        qkv_piece = exchange(qkv_parts, GROUP).reshape(8 * weight_rows, 3 * columns)
        out_halves = gather_planes(after(w_out.astype(BF16), plane_gains))
        feed_parts = after(to_units(w_gate, w_up, unit_rows), qkv_piece, out_halves)
        feed_piece = exchange(feed_parts, GROUP).reshape(8 * weight_rows, 2 * units)
        group_tokens = group_gather(after(tokens, feed_piece))
        weight_qkv = gather_planes(after(qkv_piece, plane_gains))
        weight_feed = gather_planes(feed_piece)
        weight_down = gather_planes(after(w_down.astype(BF16), feed_piece))
        out_halves = out_halves.reshape(per_head, own_heads, weight_rows, width)
        out_heads = lax.all_to_all(out_halves, head_axes, 0, 0, tiled=True)
        weight_out = out_heads.transpose(1, 0, 2, 3).reshape(columns, width)

        head_gains = gains[:2].reshape((2,) + head_shape + (HEAD,)).transpose(0, 3, 1, 2, 4)
        head_gains = lax.dynamic_index_in_dim(head_gains.reshape(2, 8, columns), member, 1, keepdims=False)
        gain_q, gain_k = head_gains.reshape(2, 1, columns)
        gain_a, gain_f = gains[2:3], gains[3:4]

        orders = [c + 4 * y + 2 * x for c in (0, 1) for y in (0, 1) for x in (0, 1)]
        starts = [(device ^ k) * rows for k in orders]

        def of_group(ids):
            return jnp.concatenate([lax.dynamic_slice_in_dim(ids, s, rows, 0) for s in starts])

        places = jnp.concatenate([s + jnp.arange(rows, dtype=jnp.int32) for s in starts])

        def by_block(array):
            shaped = array.reshape((2, blocks, group_rows // (2 * blocks)) + array.shape[1:])
            return jnp.moveaxis(shaped, 1, 0).reshape((blocks, SEQ_MAX) + array.shape[1:])

        def from_block(array):
            shaped = array.reshape((blocks, 2, SEQ_MAX // 2) + array.shape[2:])
            return jnp.moveaxis(shaped, 0, 1).reshape((group_rows,) + array.shape[2:])

        segment = by_block(of_group(segment_ids))
        piece = by_block(of_group(piece_ids))
        place_block = by_block(places) % SEQ_MAX
        before = jnp.sum((segment[:, None, :] < segment[:, :, None]).astype(jnp.int32), -1)
        positions = from_block(place_block - before)
        in_piece = (piece[:, None, :] == piece[:, :, None]) & (piece[:, :, None] > 0)
        piece_end = jnp.max(jnp.where(in_piece, place_block[:, None, :] + 1, 0), -1)
        first_seen = from_block(before).astype(F32)
        end_seen = from_block(jnp.maximum(place_block + 1, piece_end)).astype(F32)
        place = place_block[:1].astype(F32)
        freqs = jnp.exp(jnp.arange(HEAD // 2, dtype=F32) * (-2.0 * math.log(ROPE_BASE) / HEAD))
        angles = positions.astype(F32)[:, None] * freqs[None, :]
        cosine = jnp.concatenate([jnp.cos(angles), jnp.cos(angles)], 1)
        sine = jnp.concatenate([-jnp.sin(angles), jnp.sin(angles)], 1)

        projected = matmul(group_tokens, weight_qkv)
        squares = [jnp.sum(jnp.square(projected[:, i * columns : (i + 1) * columns]), -1) for i in (0, 1)]
        inverse = lax.rsqrt(group_sum(jnp.stack(squares)) / width + NORM_EPS)
        inverse = after(inverse, weight_out)
        info = jnp.stack([first_seen, end_seen, inverse[0], inverse[1]], 1)
        attention = (projected, info, cosine, sine, gain_q, gain_k, place)

        def mix(attention, weight_out):
            mixed_low = attend(*attention)
            branch = group_scatter(matmul(mixed_low, weight_out).astype(BF16), rows)
            hidden_in = tokens.astype(F32) + branch * inverse_rms(branch) * gain_a
            return mixed_low, branch, hidden_in, group_gather(hidden_in.astype(BF16))

        mixed_low, branch, hidden_in, group_hidden_in = region(mix, segment_ids, attention, weight_out)
        r_a = inverse_rms(branch)
        both, hidden = gate_up(group_hidden_in, weight_feed)
        result = group_scatter(matmul(hidden, weight_down).astype(BF16), rows)
        r_m = inverse_rms(result)
        out_tokens = (hidden_in + result * r_m * gain_f).astype(BF16)

        def norm_back(values, r, gain, grad):
            scaled = gain * grad
            mean = jnp.mean(scaled * values, -1, keepdims=True)
            return r * (scaled - values * (r * r) * mean), jnp.sum(grad * values * r, 0)

        grad_out = cotangent.astype(F32)
        result_grad, feed_gain_term = norm_back(result, r_m, gain_f, grad_out)
        group_result_grad = group_gather(result_grad.astype(BF16))

        down_term = inner_t(hidden, group_result_grad).astype(BF16)
        feed_grad = gate_up_back(after(group_result_grad, down_term), weight_down, both)
        hidden_in_parts = times_transposed(feed_grad, weight_feed)
        feed_term = inner_t(group_hidden_in, after(feed_grad, hidden_in_parts)).astype(BF16)
        down_share = scatter_planes(down_term)
        top, bottom = scatter_start(hidden_in_parts, rows, feed_term)
        feed_share = scatter_planes(feed_term)

        def to_mixer(top, bottom, branch, r_a):
            hidden_in_grad = grad_out + scatter_end(top, bottom)
            branch_grad, mixer_gain_term = norm_back(branch, r_a, gain_a, hidden_in_grad)
            return hidden_in_grad, mixer_gain_term, group_gather(branch_grad.astype(BF16))

        hidden_in_grad, mixer_gain_term, group_branch_grad = region(to_mixer, segment_ids, top, bottom, branch, r_a)
        group_branch_grad = after(group_branch_grad, down_share)
        mixed_grad = matmul_t(group_branch_grad, weight_out).astype(BF16)
        q_back, k_back, v_grad, means = attend_back(*attention, mixed_grad)
        means = group_sum(means.T).T / width
        grads, head_terms = qkv_grads(projected, q_back, k_back, v_grad, info, means, gain_q, gain_k)
        feed_back = exchange(after(feed_share, means).reshape(8, weight_rows, 2 * units), GROUP)
        grads = after(grads, feed_back)
        qkv_term = inner_t(group_tokens, grads).astype(BF16)
        qkv_share = scatter_planes(qkv_term)
        out_term = inner_t(mixed_low, after(group_branch_grad, qkv_term))
        out_parts = out_term.astype(BF16).reshape(own_heads, per_head, weight_rows, width)
        out_parts = lax.all_to_all(out_parts.transpose(1, 0, 2, 3), head_axes, 0, 0, tiled=True)
        out_share = scatter_planes(out_parts.reshape(replicas * weight_rows, width))

        def to_tokens(grads, weight_qkv, hidden_in_grad):
            return hidden_in_grad + group_scatter(matmul_t(grads, weight_qkv).astype(BF16), rows)

        g_tokens = region(to_tokens, segment_ids, after(grads, out_parts), weight_qkv, hidden_in_grad)

        qkv_back = exchange(after(qkv_share, g_tokens).reshape(8, weight_rows, 3 * columns), GROUP)
        heads_of = [
            [(e * own_heads + j) * (8 // per_head) + t for j in range(own_heads)]
            for t in range(8 // per_head)
            for e in range(per_head)
        ]
        g_qkv = from_heads(qkv_back, heads_of)
        g_w_out = out_share.astype(F32)
        g_w_down = down_share.astype(F32)
        g_w_gate, g_w_up = from_units(feed_back, unit_rows)

        head_terms = head_terms.reshape(2, 1, columns)
        spread = jnp.zeros((2, 8, columns), F32)
        spread = lax.dynamic_update_slice(spread, head_terms, (0, member, 0))
        spread = spread.reshape((2,) + head_shape_put + (HEAD,)).transpose(0, 2, 3, 1, 4)
        gain_terms = jnp.concatenate([spread.reshape(2, width), jnp.stack([mixer_gain_term, feed_gain_term])], 0)
        gain_terms = gain_terms.reshape(4, replicas, 8, weight_rows).transpose(2, 1, 0, 3)
        g_gains = halved(gain_terms.reshape(count, 4, weight_rows), GROUP + PLANES)[0]
        return (
            out_tokens,
            g_tokens,
            g_qkv[0],
            g_qkv[1],
            g_qkv[2],
            g_w_out,
            g_gains[0],
            g_gains[1],
            g_gains[2],
            g_w_gate,
            g_w_up,
            g_w_down,
            g_gains[3],
        )

    return body


def solution(mesh):
    count = mesh.shape["dev"]
    grid = Mesh(mesh.devices.reshape(count // 16, 2, 2, 2, 2), ALL)

    def run(tokens, cotangent, segment_ids, piece_ids, w_query, *rest):
        per_head = count * HEAD // w_query.shape[0]
        rows, whole, gain = P(ALL, None), P(), P(ALL)
        in_specs = (rows, rows, whole, whole) + (rows,) * 4 + (gain,) * 3 + (rows,) * 3 + (gain,)
        out_specs = (rows,) * 6 + (gain,) * 3 + (rows,) * 3 + (gain,)
        return jax.shard_map(
            make_body(count, per_head), mesh=grid, in_specs=in_specs, out_specs=out_specs, check_vma=False
        )(tokens, cotangent, segment_ids, piece_ids, w_query, *rest)

    return run
```

```python
import math

import jax
import jax.numpy as jnp
from jax import lax
from jax.experimental import pallas as pl
from jax.experimental.pallas import tpu as pltpu
from jax.sharding import Mesh, PartitionSpec as P

HEAD = 128
SEQ_MAX = 1024
NORM_EPS = 1e-06
ROPE_BASE = 500000.0
MASKED = -1e30
BF16 = jnp.bfloat16
F32 = jnp.float32
GROUP = ("y", "x", "c")
ALL = ("zh", "zl", "y", "x", "c")
PLANES = ("zh", "zl")


def matmul(left, right):
    return jnp.dot(left, right, preferred_element_type=F32)


def matmul_t(left, right):
    return lax.dot_general(left, right, (((1,), (1,)), ((), ())), preferred_element_type=F32)


def inner_t(left, right):
    return lax.dot_general(left, right, (((0,), (0,)), ((), ())), preferred_element_type=F32)


def inverse_rms(values):
    return lax.rsqrt(jnp.mean(values * values, axis=-1, keepdims=True) + NORM_EPS)


def after(value, *others):
    return lax.optimization_barrier((value,) + others)[0]


def region(function, ids, *operands):
    def nothing(*operands):
        return jax.tree.map(lambda leaf: jnp.zeros(leaf.shape, leaf.dtype), jax.eval_shape(function, *operands))

    return lax.cond(ids[0] == 0, function, nothing, *operands)


def swap(block, axis):
    return lax.ppermute(block, axis, [(0, 1), (1, 0)])


def group_gather(own):
    half = own.shape[0] // 2
    near_x = swap(own, "x")
    near_y = swap(own, "y")
    top = swap(near_x[:half], "y")
    low = swap(near_y[half:], "x")
    first = jnp.concatenate([own, near_x, near_y], 0)
    last = jnp.concatenate([top, low], 0)
    return jnp.concatenate([first, last, swap(first, "c"), swap(last, "c")], 0)


def group_sum(terms):
    total = terms.reshape(terms.shape[0], 2, 2, 2, -1)
    for dim, axis in enumerate(("c", "y", "x")):
        total = total + jnp.flip(swap(total, axis), dim + 1)
    return total.reshape(terms.shape)


def core_sum(mine, arrived):
    total = mine.astype(F32) + arrived.astype(F32)
    return total.astype(BF16).reshape(2, 2, 2, mine.shape[0] // 8, mine.shape[1])


def scatter_sends(sums):
    return sums[:, 1, 0], sums[1, :, 1]


def scatter_start(sums, sends, *others):
    got_x = after(swap(sends[0], "x"), *others)
    got_y = after(swap(sends[1], "y"), *others)
    return sums[:, 0, 0].astype(F32) + got_x.astype(F32), sums[0, :, 1].astype(F32) + got_y.astype(F32)


def scatter_end(top, bottom):
    top_last = swap(top[1].astype(BF16), "y")
    bottom_last = swap(bottom[1].astype(BF16), "x")
    return jnp.concatenate([top[0] + top_last.astype(F32), bottom[0] + bottom_last.astype(F32)], 0)


def group_scatter(mine, other):
    sums = core_sum(mine, swap(other, "c"))
    return scatter_end(*scatter_start(sums, scatter_sends(sums)))


def by_core(product, values, weight):
    half = values.shape[0] // 2
    other = product(values[half:], weight).astype(BF16)
    return product(after(values[:half], other), weight).astype(BF16), other


def doubled(own, axes):
    for axis in reversed(axes):
        size = lax.axis_size(axis)
        step = 1
        while step < size:
            got = lax.ppermute(own, axis, [(i, i ^ step) for i in range(size)])
            low_side = lax.axis_index(axis) & step == 0
            own = jnp.concatenate([jnp.where(low_side, own, got), jnp.where(low_side, got, own)], 0)
            step *= 2
    return own


def halved(terms, axes):
    for axis in axes:
        size = lax.axis_size(axis)
        step = size // 2
        while step:
            low_side = lax.axis_index(axis) & step == 0
            first, second = jnp.split(terms, 2)
            got = lax.ppermute(
                jnp.where(low_side, second, first), axis, [(i, i ^ step) for i in range(size)]
            )
            terms = jnp.where(low_side, first, second) + got
            step //= 2
    return terms


def gather_planes(part):
    return lax.all_gather(part, PLANES, axis=0, tiled=True)


def scatter_planes(term):
    return lax.psum_scatter(term, PLANES, scatter_dimension=0, tiled=True)


SCALE = HEAD ** (-0.5)
ROWS = 256
PARAMS = pltpu.CompilerParams(vmem_limit_bytes=56 * 2**20)


def flat_rows(ref):
    return ref[...].reshape(-1, ref.shape[-1])


def turn(values, cosine, sine):
    return values * cosine + pltpu.roll(values, HEAD // 2, 1) * sine


def softmax_rows(query, key, place, info):
    scores = matmul_t(query, key) * SCALE
    visible = (place >= info[:, 0:1]) & (place < info[:, 1:2])
    masked = jnp.where(visible, scores, MASKED)
    weights = jnp.exp(masked - jnp.max(masked, -1, keepdims=True))
    return weights * (1.0 / jnp.sum(weights, -1, keepdims=True))


def attend_kernel(q_ref, k_ref, v_ref, info_ref, cos_ref, sin_ref, gq_ref, gk_ref, place_ref, o_ref):
    info, cosine, sine = flat_rows(info_ref), flat_rows(cos_ref), flat_rows(sin_ref)
    query = turn(flat_rows(q_ref) * info[:, 2:3] * gq_ref[...], cosine, sine).astype(BF16)
    key = turn(flat_rows(k_ref) * info[:, 3:4] * gk_ref[...], cosine, sine).astype(BF16)
    value = flat_rows(v_ref).astype(BF16)
    place = place_ref[...]
    for start in range(0, SEQ_MAX, ROWS):
        softmax = softmax_rows(query[start : start + ROWS], key, place, info[start : start + ROWS])
        mixed = matmul(softmax.astype(BF16), value).astype(BF16)
        half, at = divmod(start, SEQ_MAX // 2)
        o_ref[half, 0, at : at + ROWS] = mixed


def attend_back_kernel(
    q_ref, k_ref, v_ref, info_ref, cos_ref, sin_ref, gq_ref, gk_ref, place_ref, do_ref,
    dq_ref, dk_ref, dv_ref, mean_ref, dk_sum, dv_sum, dq_all,
):
    info, cosine, sine = flat_rows(info_ref), flat_rows(cos_ref), flat_rows(sin_ref)
    query_in, key_in = flat_rows(q_ref), flat_rows(k_ref)
    query = turn(query_in * info[:, 2:3] * gq_ref[...], cosine, sine).astype(BF16)
    key = turn(key_in * info[:, 3:4] * gk_ref[...], cosine, sine).astype(BF16)
    value = flat_rows(v_ref).astype(BF16)
    grad = flat_rows(do_ref)
    place = place_ref[...]
    for start in range(0, SEQ_MAX, ROWS):
        part = slice(start, start + ROWS)
        softmax = softmax_rows(query[part], key, place, info[part])
        softmax_grad = matmul_t(grad[part], value)
        inner = jnp.sum(softmax * softmax_grad, -1, keepdims=True)
        score_grad = (softmax * (softmax_grad - inner)).astype(BF16)
        dq_all[part] = matmul(score_grad, key) * SCALE
        dk_term = inner_t(query[part], score_grad)
        dv_term = inner_t(grad[part], softmax.astype(BF16))
        if start:
            dk_sum[...] += dk_term
            dv_sum[...] += dv_term
        else:
            dk_sum[...] = dk_term
            dv_sum[...] = dv_term
    dq = turn(dq_all[...], cosine, -sine)
    dk = turn(dk_sum[...].T * SCALE, cosine, -sine)
    dq_ref[...] = dq.reshape(dq_ref.shape)
    dk_ref[...] = dk.reshape(dk_ref.shape)
    dv_ref[...] = dv_sum[...].T.astype(BF16).reshape(dv_ref.shape)
    mean_q = jnp.sum(dq * gq_ref[...] * query_in, -1, keepdims=True)
    mean_k = jnp.sum(dk * gk_ref[...] * key_in, -1, keepdims=True)
    mean_ref[...] = jnp.concatenate([mean_q, mean_k], 1).reshape(mean_ref.shape)


def qkv_grad_kernel(p_ref, dq_ref, dk_ref, dv_ref, info_ref, mean_ref, gq_ref, gk_ref, grads_ref, gains_ref):
    columns = dq_ref.shape[1]
    info, mean = info_ref[...], mean_ref[...]
    terms = []
    for i, (d_ref, gain_ref) in enumerate(((dq_ref, gq_ref), (dk_ref, gk_ref))):
        values, r, d = p_ref[:, i * columns : (i + 1) * columns], info[:, 2 + i : 3 + i], d_ref[...]
        grad = r * (gain_ref[...] * d - values * (r * r) * mean[:, i : i + 1])
        grads_ref[:, i * columns : (i + 1) * columns] = grad.astype(BF16)
        terms.append(jnp.sum(d * values * r, 0, keepdims=True))
    grads_ref[:, 2 * columns :] = dv_ref[...]
    term = jnp.concatenate(terms, 0)

    @pl.when(pl.program_id(0) == 0)
    def _():
        gains_ref[...] = term

    @pl.when(pl.program_id(0) > 0)
    def _():
        gains_ref[...] += term


def to_units(gate, up, unit_rows):
    rows, width = gate.shape
    units = width // 8

    def kernel(gate_ref, up_ref, out_ref):
        for i, w_ref in enumerate((gate_ref, up_ref)):
            for m in range(8):
                for r in range(units // unit_rows):
                    source, target = (r * 8 + m) * unit_rows, i * units + r * unit_rows
                    out_ref[m, :, target : target + unit_rows] = w_ref[:, source : source + unit_rows].astype(BF16)

    step = min(rows, 16)
    return pl.pallas_call(
        kernel,
        grid=(rows // step,),
        in_specs=[pl.BlockSpec((step, width), lambda i: (i, 0))] * 2,
        out_specs=pl.BlockSpec((8, step, 2 * units), lambda i: (0, i, 0)),
        out_shape=jax.ShapeDtypeStruct((8, rows, 2 * units), BF16),
        compiler_params=PARAMS,
    )(gate, up)


def from_units(parts, unit_rows):
    _, rows, units = parts.shape

    def kernel(p_ref, out_ref):
        for m in range(8):
            for r in range(units // unit_rows):
                target, source = (r * 8 + m) * unit_rows, r * unit_rows
                out_ref[:, target : target + unit_rows] = p_ref[m, :, source : source + unit_rows].astype(F32)

    step = min(rows, 16)
    return pl.pallas_call(
        kernel,
        grid=(rows // step,),
        in_specs=[pl.BlockSpec((8, step, units), lambda i: (0, i, 0))],
        out_specs=pl.BlockSpec((step, 8 * units), lambda i: (i, 0)),
        out_shape=jax.ShapeDtypeStruct((rows, 8 * units), F32),
        compiler_params=PARAMS,
    )(parts)


def from_heads(parts, members):
    _, rows, columns = parts.shape
    columns //= 3

    def kernel(p_ref, *out_refs):
        for i, out_ref in enumerate(out_refs):
            for m, targets in enumerate(members):
                for j, head in enumerate(targets):
                    source = i * columns + j * HEAD
                    out_ref[:, head * HEAD : (head + 1) * HEAD] = p_ref[m, :, source : source + HEAD].astype(F32)

    step = min(rows, 16)
    return pl.pallas_call(
        kernel,
        grid=(rows // step,),
        in_specs=[pl.BlockSpec((8, step, 3 * columns), lambda i: (0, i, 0))],
        out_specs=[pl.BlockSpec((step, 8 * columns), lambda i: (i, 0))] * 3,
        out_shape=[jax.ShapeDtypeStruct((rows, 8 * columns), F32)] * 3,
        compiler_params=PARAMS,
    )(parts)


def whole(array):
    return pl.BlockSpec(array.shape, lambda i: (0, 0), pipeline_mode=pl.Buffered(1))


def by_rows(step, width):
    return pl.BlockSpec((step, width), lambda i: (i, 0))


def gate_up(values, weight):
    rows, depth = values.shape
    units = weight.shape[1] // 2

    def kernel(v_ref, w_ref, both_ref, hidden_ref):
        for c in range(0, units, 512):
            gate = matmul(v_ref[...], w_ref[:, c : c + 512])
            up = matmul(v_ref[...], w_ref[:, units + c : units + c + 512])
            both_ref[:, c : c + 512] = gate
            both_ref[:, units + c : units + c + 512] = up
            hidden_ref[:, c : c + 512] = (gate / (1.0 + jnp.exp(-gate)) * up).astype(BF16)

    return pl.pallas_call(
        kernel,
        grid=(rows // ROWS,),
        in_specs=[by_rows(ROWS, depth), whole(weight)],
        out_specs=[by_rows(ROWS, 2 * units), by_rows(ROWS, units)],
        out_shape=[jax.ShapeDtypeStruct((rows, 2 * units), F32), jax.ShapeDtypeStruct((rows, units), BF16)],
        compiler_params=PARAMS,
        cost_estimate=pl.CostEstimate(
            flops=4 * rows * depth * units, bytes_accessed=14 * rows * units, transcendentals=rows * units
        ),
    )(values, weight)


def gate_up_back(grad, weight, both):
    rows, depth = grad.shape
    units = weight.shape[0]

    def kernel(g_ref, w_ref, both_ref, out_ref):
        for c in range(0, units, 512):
            hidden_grad = matmul_t(g_ref[...], w_ref[c : c + 512, :])
            gate, up = both_ref[:, c : c + 512], both_ref[:, units + c : units + c + 512]
            sig = 1.0 / (1.0 + jnp.exp(-gate))
            out_ref[:, c : c + 512] = (hidden_grad * up * sig * (1.0 + gate * (1.0 - sig))).astype(BF16)
            out_ref[:, units + c : units + c + 512] = (hidden_grad * (gate * sig)).astype(BF16)

    return pl.pallas_call(
        kernel,
        grid=(rows // ROWS,),
        in_specs=[by_rows(ROWS, depth), whole(weight), by_rows(ROWS, 2 * units)],
        out_specs=by_rows(ROWS, 2 * units),
        out_shape=jax.ShapeDtypeStruct((rows, 2 * units), BF16),
        compiler_params=PARAMS,
        cost_estimate=pl.CostEstimate(
            flops=2 * rows * depth * units, bytes_accessed=16 * rows * units, transcendentals=rows * units
        ),
    )(grad, weight, both)


def times_transposed(values, weight, first, rows):
    depth, width = values.shape[1], weight.shape[0]

    def kernel(v_ref, w_ref, out_ref):
        for c in range(0, width, 512):
            out_ref[:, c : c + 512] = matmul_t(v_ref[...], w_ref[c : c + 512, :]).astype(BF16)

    return pl.pallas_call(
        kernel,
        grid=(rows // ROWS,),
        in_specs=[pl.BlockSpec((ROWS, depth), lambda i: (first // ROWS + i, 0)), whole(weight)],
        out_specs=by_rows(ROWS, width),
        out_shape=jax.ShapeDtypeStruct((rows, width), BF16),
        compiler_params=PARAMS,
        cost_estimate=pl.CostEstimate(
            flops=2 * rows * depth * width, bytes_accessed=2 * rows * (depth + width), transcendentals=0
        ),
    )(values, weight)


def head_specs(heads):
    def of(width, column):
        return pl.BlockSpec((2, 1, SEQ_MAX // 2, width), lambda b, h: (0, b, 0, column(h)))

    gain = pl.BlockSpec((1, HEAD), lambda b, h: (0, h))
    return of, [
        of(HEAD, lambda h: h),
        of(HEAD, lambda h: heads + h),
        of(HEAD, lambda h: 2 * heads + h),
        of(4, lambda h: 0),
        of(HEAD, lambda h: 0),
        of(HEAD, lambda h: 0),
        gain,
        gain,
        pl.BlockSpec((1, SEQ_MAX), lambda b, h: (0, 0)),
    ]


def in_blocks(array):
    return array.reshape(2, -1, SEQ_MAX // 2, array.shape[-1])


def attend(projected, info, cosine, sine, gain_q, gain_k, place):
    rows, columns = projected.shape[0], projected.shape[1] // 3
    heads, blocks = columns // HEAD, rows // SEQ_MAX
    of, specs = head_specs(heads)
    p = in_blocks(projected)
    mixed = pl.pallas_call(
        attend_kernel,
        grid=(blocks, heads),
        in_specs=specs,
        out_specs=of(HEAD, lambda h: h),
        out_shape=jax.ShapeDtypeStruct((2, blocks, SEQ_MAX // 2, columns), BF16),
        compiler_params=PARAMS,
        cost_estimate=pl.CostEstimate(
            flops=4 * rows * SEQ_MAX * columns, bytes_accessed=8 * rows * columns * 2, transcendentals=rows * SEQ_MAX * heads
        ),
    )(p, p, p, in_blocks(info), in_blocks(cosine), in_blocks(sine), gain_q, gain_k, place)
    return mixed.reshape(rows, columns)


def attend_back(projected, info, cosine, sine, gain_q, gain_k, place, mixed_grad):
    rows, columns = projected.shape[0], projected.shape[1] // 3
    heads, blocks = columns // HEAD, rows // SEQ_MAX
    of, specs = head_specs(heads)
    p = in_blocks(projected)
    shape = (2, blocks, SEQ_MAX // 2, columns)
    dq, dk, dv, means = pl.pallas_call(
        attend_back_kernel,
        grid=(blocks, heads),
        in_specs=specs + [of(HEAD, lambda h: h)],
        out_specs=[of(HEAD, lambda h: h)] * 3
        + [pl.BlockSpec((1, 2, 1, SEQ_MAX // 2, 2), lambda b, h: (h, 0, b, 0, 0))],
        out_shape=[
            jax.ShapeDtypeStruct(shape, F32),
            jax.ShapeDtypeStruct(shape, F32),
            jax.ShapeDtypeStruct(shape, BF16),
            jax.ShapeDtypeStruct((heads,) + shape[:3] + (2,), F32),
        ],
        scratch_shapes=[pltpu.VMEM((HEAD, SEQ_MAX), F32)] * 2 + [pltpu.VMEM((SEQ_MAX, HEAD), F32)],
        compiler_params=PARAMS,
        cost_estimate=pl.CostEstimate(
            flops=10 * rows * SEQ_MAX * columns, bytes_accessed=12 * rows * columns * 2, transcendentals=rows * SEQ_MAX * heads
        ),
    )(p, p, p, in_blocks(info), in_blocks(cosine), in_blocks(sine), gain_q, gain_k, place, in_blocks(mixed_grad))
    flat = [array.reshape(rows, columns) for array in (dq, dk, dv)]
    return *flat, jnp.sum(means, 0).reshape(rows, 2)


def qkv_grads(projected, dq, dk, dv, info, mean, gain_q, gain_k):
    rows, columns = dq.shape
    step = 512

    def by_row(width):
        return pl.BlockSpec((step, width), lambda i: (i, 0))

    def fixed(height):
        return pl.BlockSpec((height, columns), lambda i: (0, 0))

    return pl.pallas_call(
        qkv_grad_kernel,
        grid=(rows // step,),
        in_specs=[by_row(3 * columns)] + [by_row(columns)] * 3 + [by_row(4), by_row(2), fixed(1), fixed(1)],
        out_specs=[by_row(3 * columns), fixed(2)],
        out_shape=[
            jax.ShapeDtypeStruct((rows, 3 * columns), BF16),
            jax.ShapeDtypeStruct((2, columns), F32),
        ],
        compiler_params=PARAMS,
    )(projected, dq, dk, dv, info, mean, gain_q, gain_k)


def make_body(count, per_head):
    replicas = count // 8
    own_heads = replicas // per_head
    head_axes = GROUP[3 - int(math.log2(per_head)) :]
    head_shape = (per_head, own_heads, 8 // per_head)
    head_shape_put = (8 // per_head, per_head, own_heads)

    def body(
        tokens,
        cotangent,
        segment_ids,
        piece_ids,
        w_query,
        w_key,
        w_value,
        w_out,
        query_gain,
        key_gain,
        mixer_gain,
        w_gate,
        w_up,
        w_down,
        feed_gain,
    ):
        rows, width = tokens.shape
        weight_rows = w_query.shape[0]
        unit_rows = w_down.shape[0]
        units = replicas * unit_rows
        columns = own_heads * HEAD
        group_rows = 8 * rows
        blocks = group_rows // SEQ_MAX
        member = lax.axis_index(GROUP)
        device = lax.axis_index(ALL)

        def by_head(weight):
            shaped = weight.astype(BF16).reshape((weight_rows,) + head_shape + (HEAD,))
            return shaped.transpose(3, 1, 0, 2, 4).reshape(8, weight_rows, columns)

        def exchange(parts, group):
            return lax.all_to_all(parts, group, 0, 0, tiled=True)

        own_gains = jnp.stack([query_gain, key_gain, mixer_gain, feed_gain]).astype(BF16)
        plane_gains = doubled(own_gains.reshape(1, 4, weight_rows), PLANES)
        gains = doubled(plane_gains, GROUP).reshape(8, replicas, 4, weight_rows)
        gains = gains.transpose(2, 1, 0, 3).reshape(4, width).astype(F32)

        qkv_parts = jnp.concatenate([by_head(w_query), by_head(w_key), by_head(w_value)], 2)
        qkv_piece = exchange(qkv_parts, GROUP).reshape(8 * weight_rows, 3 * columns)
        out_halves = gather_planes(after(w_out.astype(BF16), plane_gains))
        feed_parts = after(to_units(w_gate, w_up, unit_rows), qkv_piece, out_halves)
        feed_piece = exchange(feed_parts, GROUP).reshape(8 * weight_rows, 2 * units)
        group_tokens = group_gather(after(tokens, feed_piece))
        weight_qkv = gather_planes(after(qkv_piece, plane_gains))
        weight_feed = gather_planes(feed_piece)
        weight_down = gather_planes(after(w_down.astype(BF16), feed_piece))
        out_halves = out_halves.reshape(per_head, own_heads, weight_rows, width)
        out_heads = lax.all_to_all(out_halves, head_axes, 0, 0, tiled=True)
        weight_out = out_heads.transpose(1, 0, 2, 3).reshape(columns, width)

        head_gains = gains[:2].reshape((2,) + head_shape + (HEAD,)).transpose(0, 3, 1, 2, 4)
        head_gains = lax.dynamic_index_in_dim(head_gains.reshape(2, 8, columns), member, 1, keepdims=False)
        gain_q, gain_k = head_gains.reshape(2, 1, columns)
        gain_a, gain_f = gains[2:3], gains[3:4]

        orders = [c + 4 * y + 2 * x for c in (0, 1) for y in (0, 1) for x in (0, 1)]
        starts = [(device ^ k) * rows for k in orders]

        def of_group(ids):
            return jnp.concatenate([lax.dynamic_slice_in_dim(ids, s, rows, 0) for s in starts])

        places = jnp.concatenate([s + jnp.arange(rows, dtype=jnp.int32) for s in starts])

        def by_block(array):
            shaped = array.reshape((2, blocks, group_rows // (2 * blocks)) + array.shape[1:])
            return jnp.moveaxis(shaped, 1, 0).reshape((blocks, SEQ_MAX) + array.shape[1:])

        def from_block(array):
            shaped = array.reshape((blocks, 2, SEQ_MAX // 2) + array.shape[2:])
            return jnp.moveaxis(shaped, 0, 1).reshape((group_rows,) + array.shape[2:])

        segment = by_block(of_group(segment_ids))
        piece = by_block(of_group(piece_ids))
        place_block = by_block(places) % SEQ_MAX
        before = jnp.sum((segment[:, None, :] < segment[:, :, None]).astype(jnp.int32), -1)
        positions = from_block(place_block - before)
        in_piece = (piece[:, None, :] == piece[:, :, None]) & (piece[:, :, None] > 0)
        piece_end = jnp.max(jnp.where(in_piece, place_block[:, None, :] + 1, 0), -1)
        first_seen = from_block(before).astype(F32)
        end_seen = from_block(jnp.maximum(place_block + 1, piece_end)).astype(F32)
        place = place_block[:1].astype(F32)
        freqs = jnp.exp(jnp.arange(HEAD // 2, dtype=F32) * (-2.0 * math.log(ROPE_BASE) / HEAD))
        angles = positions.astype(F32)[:, None] * freqs[None, :]
        cosine = jnp.concatenate([jnp.cos(angles), jnp.cos(angles)], 1)
        sine = jnp.concatenate([-jnp.sin(angles), jnp.sin(angles)], 1)

        projected = matmul(group_tokens, weight_qkv)
        squares = [jnp.sum(jnp.square(projected[:, i * columns : (i + 1) * columns]), -1) for i in (0, 1)]
        inverse = lax.rsqrt(group_sum(jnp.stack(squares)) / width + NORM_EPS)
        inverse = after(inverse, weight_out)
        info = lax.optimization_barrier(jnp.stack([first_seen, end_seen, inverse[0], inverse[1]], 1))
        attention = (projected, info, cosine, sine, gain_q, gain_k, place)

        def mix(attention, weight_out):
            mixed_low = attend(*attention)
            branch = group_scatter(*by_core(matmul, mixed_low, weight_out))
            hidden_in = tokens.astype(F32) + branch * inverse_rms(branch) * gain_a
            return mixed_low, branch, hidden_in, group_gather(hidden_in.astype(BF16))

        mixed_low, branch, hidden_in, group_hidden_in = region(mix, segment_ids, attention, weight_out)
        r_a = inverse_rms(branch)
        both, hidden = gate_up(group_hidden_in, weight_feed)
        result = group_scatter(*by_core(matmul, hidden, weight_down))
        r_m = inverse_rms(result)
        out_tokens = (hidden_in + result * r_m * gain_f).astype(BF16)

        def norm_back(values, r, gain, grad):
            scaled = gain * grad
            mean = jnp.mean(scaled * values, -1, keepdims=True)
            return r * (scaled - values * (r * r) * mean), jnp.sum(grad * values * r, 0)

        grad_out = cotangent.astype(F32)
        result_grad, feed_gain_term = norm_back(result, r_m, gain_f, grad_out)
        group_result_grad = group_gather(result_grad.astype(BF16))

        down_term = inner_t(hidden, group_result_grad).astype(BF16)
        down_share = scatter_planes(down_term)

        def feed_mix(group_result_grad, weight_down, weight_feed, both, group_hidden_in):
            feed_grad = gate_up_back(group_result_grad, weight_down, both)
            half = group_rows // 2
            for_other = times_transposed(feed_grad, weight_feed, half, half)
            arrived = swap(for_other, "c")
            for_mine = times_transposed(after(feed_grad, for_other), weight_feed, 0, half)
            sums = core_sum(for_mine, arrived)
            sends = lax.optimization_barrier(scatter_sends(sums))
            ready = after(feed_grad, *sends)
            gate_term = inner_t(group_hidden_in, ready[:, :units]).astype(BF16)
            up_term = inner_t(group_hidden_in, ready[:, units:]).astype(BF16)
            return gate_term, up_term, *scatter_start(sums, sends, gate_term, up_term)

        gate_term, up_term, top, bottom = region(
            feed_mix, segment_ids, after(group_result_grad, down_term), weight_down, weight_feed, both, group_hidden_in
        )
        gate_share = scatter_planes(gate_term)
        up_share = scatter_planes(up_term)

        def to_mixer(top, bottom, branch, r_a):
            hidden_in_grad = grad_out + scatter_end(top, bottom)
            branch_grad, mixer_gain_term = norm_back(branch, r_a, gain_a, hidden_in_grad)
            return hidden_in_grad, mixer_gain_term, group_gather(branch_grad.astype(BF16))

        hidden_in_grad, mixer_gain_term, group_branch_grad = region(to_mixer, segment_ids, top, bottom, branch, r_a)
        group_branch_grad = after(group_branch_grad, down_share)
        mixed_grad = matmul_t(group_branch_grad, weight_out).astype(BF16)
        q_back, k_back, v_grad, means = attend_back(*attention, mixed_grad)
        gate_back = exchange(after(gate_share, group_branch_grad).reshape(8, weight_rows, units), GROUP)
        means = group_sum(after(means, gate_back).T).T / width
        grads, head_terms = qkv_grads(projected, q_back, k_back, v_grad, info, means, gain_q, gain_k)
        up_back = exchange(after(up_share, means).reshape(8, weight_rows, units), GROUP)
        qkv_term = inner_t(group_tokens, grads).astype(BF16)
        qkv_share = scatter_planes(qkv_term)
        out_term = inner_t(mixed_low, after(group_branch_grad, qkv_term, up_share))
        out_parts = out_term.astype(BF16).reshape(own_heads, per_head, weight_rows, width)
        out_parts = lax.all_to_all(out_parts.transpose(1, 0, 2, 3), head_axes, 0, 0, tiled=True)
        out_share = scatter_planes(out_parts.reshape(replicas * weight_rows, width))

        head_terms = head_terms.reshape(2, 1, columns)
        spread = jnp.zeros((2, 8, columns), F32)
        spread = lax.dynamic_update_slice(spread, head_terms, (0, member, 0))
        spread = spread.reshape((2,) + head_shape_put + (HEAD,)).transpose(0, 2, 3, 1, 4)
        gain_terms = jnp.concatenate([spread.reshape(2, width), jnp.stack([mixer_gain_term, feed_gain_term])], 0)
        gain_terms = gain_terms.reshape(4, replicas, 8, weight_rows).transpose(2, 1, 0, 3)
        gain_terms = gain_terms.reshape(count, 4, weight_rows)

        def to_tokens(grads, weight_qkv, gain_terms, gate_back, down_share):
            mine, other = by_core(matmul_t, grads, weight_qkv)
            sums = core_sum(mine, swap(other, "c"))
            sends = scatter_sends(sums)
            done = halved(gain_terms, GROUP), from_units(gate_back, unit_rows), down_share.astype(F32)
            return scatter_start(sums, sends), *done

        token_sums, gain_terms, g_w_gate, g_w_down = region(
            to_tokens, segment_ids, after(grads, out_parts), weight_qkv, gain_terms, gate_back, down_share
        )
        g_gains = halved(gain_terms, PLANES)[0]
        qkv_back = exchange(after(qkv_share, *token_sums, up_back).reshape(8, weight_rows, 3 * columns), GROUP)
        top, bottom = token_sums
        g_tokens = hidden_in_grad + scatter_end(after(top, qkv_back), after(bottom, qkv_back))
        heads_of = [
            [(e * own_heads + j) * (8 // per_head) + t for j in range(own_heads)]
            for t in range(8 // per_head)
            for e in range(per_head)
        ]
        g_qkv = from_heads(qkv_back, heads_of)
        g_w_out = out_share.astype(F32)
        g_w_up = from_units(after(up_back, token_sums[0]), unit_rows)

        return (
            out_tokens,
            g_tokens,
            g_qkv[0],
            g_qkv[1],
            g_qkv[2],
            g_w_out,
            g_gains[0],
            g_gains[1],
            g_gains[2],
            g_w_gate,
            g_w_up,
            g_w_down,
            g_gains[3],
        )

    return body


def solution(mesh):
    count = mesh.shape["dev"]
    grid = Mesh(mesh.devices.reshape(count // 16, 2, 2, 2, 2), ALL)

    def run(tokens, cotangent, segment_ids, piece_ids, w_query, *rest):
        per_head = count * HEAD // w_query.shape[0]
        rows, whole, gain = P(ALL, None), P(), P(ALL)
        in_specs = (rows, rows, whole, whole) + (rows,) * 4 + (gain,) * 3 + (rows,) * 3 + (gain,)
        out_specs = (rows,) * 6 + (gain,) * 3 + (rows,) * 3 + (gain,)
        return jax.shard_map(
            make_body(count, per_head), mesh=grid, in_specs=in_specs, out_specs=out_specs, check_vma=False
        )(tokens, cotangent, segment_ids, piece_ids, w_query, *rest)

    return run
```

```python
import math

import jax
import jax.numpy as jnp
from jax import lax
from jax.experimental import pallas as pl
from jax.experimental.pallas import tpu as pltpu
from jax.sharding import Mesh, PartitionSpec as P

HEAD = 128
SEQ_MAX = 1024
NORM_EPS = 1e-06
ROPE_BASE = 500000.0
MASKED = -1e30
BF16 = jnp.bfloat16
F32 = jnp.float32
GROUP = ("y", "x", "c")
ALL = ("zh", "zl", "y", "x", "c")
PLANES = ("zh", "zl")


def matmul(left, right):
    return jnp.dot(left, right, preferred_element_type=F32)


def matmul_t(left, right):
    return lax.dot_general(left, right, (((1,), (1,)), ((), ())), preferred_element_type=F32)


def inner_t(left, right):
    return lax.dot_general(left, right, (((0,), (0,)), ((), ())), preferred_element_type=F32)


def inverse_rms(values):
    return lax.rsqrt(jnp.mean(values * values, axis=-1, keepdims=True) + NORM_EPS)


def after(value, *others):
    return lax.optimization_barrier((value,) + others)[0]


def region(function, ids, *operands):
    def nothing(*operands):
        return jax.tree.map(lambda leaf: jnp.zeros(leaf.shape, leaf.dtype), jax.eval_shape(function, *operands))

    return lax.cond(ids[0] == 0, function, nothing, *operands)


def swap(block, axis):
    return lax.ppermute(block, axis, [(0, 1), (1, 0)])


def group_gather(own):
    half = own.shape[0] // 2
    near_x = swap(own, "x")
    near_y = swap(own, "y")
    top = swap(near_x[:half], "y")
    low = swap(near_y[half:], "x")
    first = jnp.concatenate([own, near_x, near_y], 0)
    blocks = lax.optimization_barrier(jnp.concatenate([first, own, swap(first, "c"), own], 0))
    last = jnp.concatenate([after(top, blocks), after(low, blocks)], 0)
    last_other = swap(last, "c")
    blocks = lax.dynamic_update_slice(blocks, last, (3 * 2 * half, 0))
    return lax.dynamic_update_slice(blocks, last_other, (7 * 2 * half, 0))


def group_sum(terms):
    total = terms.reshape(terms.shape[0], 2, 2, 2, -1)
    for dim, axis in enumerate(("c", "y", "x")):
        total = total + jnp.flip(swap(total, axis), dim + 1)
    return total.reshape(terms.shape)


def core_sum(mine, arrived):
    total = mine.astype(F32) + arrived.astype(F32)
    return total.astype(BF16).reshape(2, 2, 2, mine.shape[0] // 8, mine.shape[1])


def scatter_sends(sums):
    return sums[:, 1, 0], sums[1, :, 1]


def scatter_start(sums, sends, *others):
    got_x = after(swap(sends[0], "x"), *others)
    got_y = after(swap(sends[1], "y"), *others)
    return sums[:, 0, 0].astype(F32) + got_x.astype(F32), sums[0, :, 1].astype(F32) + got_y.astype(F32)


def scatter_end(top, bottom):
    top_last = swap(top[1].astype(BF16), "y")
    bottom_last = swap(bottom[1].astype(BF16), "x")
    return jnp.concatenate([top[0] + top_last.astype(F32), bottom[0] + bottom_last.astype(F32)], 0)


def group_scatter(mine, other):
    sums = core_sum(mine, swap(other, "c"))
    return scatter_end(*scatter_start(sums, scatter_sends(sums)))


def by_core(product, values, weight):
    half = values.shape[0] // 2
    other = product(values[half:], weight).astype(BF16)
    return product(after(values[:half], other), weight).astype(BF16), other


def doubled(own, axes):
    for axis in reversed(axes):
        size = lax.axis_size(axis)
        step = 1
        while step < size:
            got = lax.ppermute(own, axis, [(i, i ^ step) for i in range(size)])
            low_side = lax.axis_index(axis) & step == 0
            own = jnp.concatenate([jnp.where(low_side, own, got), jnp.where(low_side, got, own)], 0)
            step *= 2
    return own


def halved(terms, axes):
    for axis in axes:
        size = lax.axis_size(axis)
        step = size // 2
        while step:
            low_side = lax.axis_index(axis) & step == 0
            first, second = jnp.split(terms, 2)
            got = lax.ppermute(
                jnp.where(low_side, second, first), axis, [(i, i ^ step) for i in range(size)]
            )
            terms = jnp.where(low_side, first, second) + got
            step //= 2
    return terms


def gather_planes(part):
    return lax.all_gather(part, PLANES, axis=0, tiled=True)


def scatter_planes(term):
    return lax.psum_scatter(term, PLANES, scatter_dimension=0, tiled=True)


SCALE = HEAD ** (-0.5)
ROWS = 256
FEED_ROWS = 512
PARAMS = pltpu.CompilerParams(vmem_limit_bytes=56 * 2**20)


def flat_rows(ref):
    return ref[...].reshape(-1, ref.shape[-1])


def turn(values, cosine, sine):
    return values * cosine + pltpu.roll(values, HEAD // 2, 1) * sine


def softmax_rows(query, key, place, info):
    scores = matmul_t(query, key) * SCALE
    visible = (place >= info[:, 0:1]) & (place < info[:, 1:2])
    masked = jnp.where(visible, scores, MASKED)
    weights = jnp.exp(masked - jnp.max(masked, -1, keepdims=True))
    return weights * (1.0 / jnp.sum(weights, -1, keepdims=True))


def attend_kernel(q_ref, k_ref, v_ref, info_ref, cos_ref, sin_ref, gq_ref, gk_ref, place_ref, o_ref):
    info, cosine, sine = flat_rows(info_ref), flat_rows(cos_ref), flat_rows(sin_ref)
    query = turn(flat_rows(q_ref) * info[:, 2:3] * gq_ref[...], cosine, sine).astype(BF16)
    key = turn(flat_rows(k_ref) * info[:, 3:4] * gk_ref[...], cosine, sine).astype(BF16)
    value = flat_rows(v_ref).astype(BF16)
    place = place_ref[...]
    for start in range(0, SEQ_MAX, ROWS):
        softmax = softmax_rows(query[start : start + ROWS], key, place, info[start : start + ROWS])
        mixed = matmul(softmax.astype(BF16), value).astype(BF16)
        half, at = divmod(start, SEQ_MAX // 2)
        o_ref[half, 0, at : at + ROWS] = mixed


def attend_back_kernel(
    q_ref, k_ref, v_ref, info_ref, cos_ref, sin_ref, gq_ref, gk_ref, place_ref, do_ref,
    dq_ref, dk_ref, dv_ref, mean_ref, dk_sum, dv_sum, dq_all,
):
    info, cosine, sine = flat_rows(info_ref), flat_rows(cos_ref), flat_rows(sin_ref)
    query_in, key_in = flat_rows(q_ref), flat_rows(k_ref)
    query = turn(query_in * info[:, 2:3] * gq_ref[...], cosine, sine).astype(BF16)
    key = turn(key_in * info[:, 3:4] * gk_ref[...], cosine, sine).astype(BF16)
    value = flat_rows(v_ref).astype(BF16)
    grad = flat_rows(do_ref)
    place = place_ref[...]
    for start in range(0, SEQ_MAX, ROWS):
        part = slice(start, start + ROWS)
        softmax = softmax_rows(query[part], key, place, info[part])
        softmax_grad = matmul_t(grad[part], value)
        inner = jnp.sum(softmax * softmax_grad, -1, keepdims=True)
        score_grad = (softmax * (softmax_grad - inner)).astype(BF16)
        dq_all[part] = matmul(score_grad, key) * SCALE
        dk_term = inner_t(query[part], score_grad)
        dv_term = inner_t(grad[part], softmax.astype(BF16))
        if start:
            dk_sum[...] += dk_term
            dv_sum[...] += dv_term
        else:
            dk_sum[...] = dk_term
            dv_sum[...] = dv_term
    dq = turn(dq_all[...], cosine, -sine)
    dk = turn(dk_sum[...].T * SCALE, cosine, -sine)
    dq_ref[...] = dq.reshape(dq_ref.shape)
    dk_ref[...] = dk.reshape(dk_ref.shape)
    dv_ref[...] = dv_sum[...].T.astype(BF16).reshape(dv_ref.shape)
    mean_q = jnp.sum(dq * gq_ref[...] * query_in, -1, keepdims=True)
    mean_k = jnp.sum(dk * gk_ref[...] * key_in, -1, keepdims=True)
    mean_ref[...] = jnp.concatenate([mean_q, mean_k], 1).reshape(mean_ref.shape)


def qkv_grad_kernel(p_ref, dq_ref, dk_ref, dv_ref, info_ref, mean_ref, gq_ref, gk_ref, grads_ref, gains_ref):
    columns = dq_ref.shape[1]
    info, mean = info_ref[...], mean_ref[...]
    terms = []
    for i, (d_ref, gain_ref) in enumerate(((dq_ref, gq_ref), (dk_ref, gk_ref))):
        values, r, d = p_ref[:, i * columns : (i + 1) * columns], info[:, 2 + i : 3 + i], d_ref[...]
        grad = r * (gain_ref[...] * d - values * (r * r) * mean[:, i : i + 1])
        grads_ref[:, i * columns : (i + 1) * columns] = grad.astype(BF16)
        terms.append(jnp.sum(d * values * r, 0, keepdims=True))
    grads_ref[:, 2 * columns :] = dv_ref[...]
    term = jnp.concatenate(terms, 0)

    @pl.when(pl.program_id(0) == 0)
    def _():
        gains_ref[...] = term

    @pl.when(pl.program_id(0) > 0)
    def _():
        gains_ref[...] += term


def to_units(gate, up, unit_rows):
    rows, width = gate.shape
    units = width // 8

    def kernel(gate_ref, up_ref, out_ref):
        for i, w_ref in enumerate((gate_ref, up_ref)):
            for m in range(8):
                for r in range(units // unit_rows):
                    source, target = (r * 8 + m) * unit_rows, i * units + r * unit_rows
                    out_ref[m, :, target : target + unit_rows] = w_ref[:, source : source + unit_rows].astype(BF16)

    step = min(rows, 16)
    return pl.pallas_call(
        kernel,
        grid=(rows // step,),
        in_specs=[pl.BlockSpec((step, width), lambda i: (i, 0))] * 2,
        out_specs=pl.BlockSpec((8, step, 2 * units), lambda i: (0, i, 0)),
        out_shape=jax.ShapeDtypeStruct((8, rows, 2 * units), BF16),
        compiler_params=PARAMS,
    )(gate, up)


def from_units(parts, unit_rows):
    _, rows, units = parts.shape
    units //= 2

    def kernel(p_ref, *out_refs):
        for i, out_ref in enumerate(out_refs):
            for m in range(8):
                for r in range(units // unit_rows):
                    target, source = (r * 8 + m) * unit_rows, i * units + r * unit_rows
                    out_ref[:, target : target + unit_rows] = p_ref[m, :, source : source + unit_rows].astype(F32)

    step = min(rows, 16)
    return pl.pallas_call(
        kernel,
        grid=(rows // step,),
        in_specs=[pl.BlockSpec((8, step, 2 * units), lambda i: (0, i, 0))],
        out_specs=[pl.BlockSpec((step, 8 * units), lambda i: (i, 0))] * 2,
        out_shape=[jax.ShapeDtypeStruct((rows, 8 * units), F32)] * 2,
        compiler_params=PARAMS,
    )(parts)


def from_heads(parts, members):
    _, rows, columns = parts.shape
    columns //= 3

    def kernel(p_ref, *out_refs):
        for i, out_ref in enumerate(out_refs):
            for m, targets in enumerate(members):
                for j, head in enumerate(targets):
                    source = i * columns + j * HEAD
                    out_ref[:, head * HEAD : (head + 1) * HEAD] = p_ref[m, :, source : source + HEAD].astype(F32)

    step = min(rows, 16)
    return pl.pallas_call(
        kernel,
        grid=(rows // step,),
        in_specs=[pl.BlockSpec((8, step, 3 * columns), lambda i: (0, i, 0))],
        out_specs=[pl.BlockSpec((step, 8 * columns), lambda i: (i, 0))] * 3,
        out_shape=[jax.ShapeDtypeStruct((rows, 8 * columns), F32)] * 3,
        compiler_params=PARAMS,
    )(parts)


def whole(array):
    return pl.BlockSpec(array.shape, lambda i: (0, 0), pipeline_mode=pl.Buffered(1))


def by_rows(step, width):
    return pl.BlockSpec((step, width), lambda i: (i, 0))


def gate_up(values, weight):
    rows, depth = values.shape
    units = weight.shape[1] // 2

    def kernel(v_ref, w_ref, both_ref, hidden_ref):
        for c in range(0, units, 512):
            gate = matmul(v_ref[...], w_ref[:, c : c + 512])
            up = matmul(v_ref[...], w_ref[:, units + c : units + c + 512])
            both_ref[:, c : c + 512] = gate
            both_ref[:, units + c : units + c + 512] = up
            hidden_ref[:, c : c + 512] = (gate / (1.0 + jnp.exp(-gate)) * up).astype(BF16)

    return pl.pallas_call(
        kernel,
        grid=(rows // ROWS,),
        in_specs=[by_rows(ROWS, depth), whole(weight)],
        out_specs=[by_rows(ROWS, 2 * units), by_rows(ROWS, units)],
        out_shape=[jax.ShapeDtypeStruct((rows, 2 * units), F32), jax.ShapeDtypeStruct((rows, units), BF16)],
        compiler_params=PARAMS,
        cost_estimate=pl.CostEstimate(
            flops=4 * rows * depth * units, bytes_accessed=14 * rows * units, transcendentals=rows * units
        ),
    )(values, weight)


def gate_up_back(grad, weight, both):
    rows, depth = grad.shape
    units = weight.shape[0]

    def kernel(g_ref, w_ref, both_ref, out_ref):
        for c in range(0, units, 512):
            hidden_grad = matmul_t(g_ref[...], w_ref[c : c + 512, :])
            gate, up = both_ref[:, c : c + 512], both_ref[:, units + c : units + c + 512]
            sig = 1.0 / (1.0 + jnp.exp(-gate))
            out_ref[:, c : c + 512] = (hidden_grad * up * sig * (1.0 + gate * (1.0 - sig))).astype(BF16)
            out_ref[:, units + c : units + c + 512] = (hidden_grad * (gate * sig)).astype(BF16)

    return pl.pallas_call(
        kernel,
        grid=(rows // FEED_ROWS,),
        in_specs=[by_rows(FEED_ROWS, depth), whole(weight), by_rows(FEED_ROWS, 2 * units)],
        out_specs=by_rows(FEED_ROWS, 2 * units),
        out_shape=jax.ShapeDtypeStruct((rows, 2 * units), BF16),
        compiler_params=PARAMS,
        cost_estimate=pl.CostEstimate(
            flops=2 * rows * depth * units, bytes_accessed=16 * rows * units, transcendentals=rows * units
        ),
    )(grad, weight, both)


def times_transposed(values, weight, first, rows):
    depth, width = values.shape[1], weight.shape[0]

    def kernel(v_ref, w_ref, out_ref):
        for c in range(0, width, 512):
            out_ref[:, c : c + 512] = matmul_t(v_ref[...], w_ref[c : c + 512, :]).astype(BF16)

    return pl.pallas_call(
        kernel,
        grid=(rows // FEED_ROWS,),
        in_specs=[pl.BlockSpec((FEED_ROWS, depth), lambda i: (first // FEED_ROWS + i, 0)), whole(weight)],
        out_specs=by_rows(FEED_ROWS, width),
        out_shape=jax.ShapeDtypeStruct((rows, width), BF16),
        compiler_params=PARAMS,
        cost_estimate=pl.CostEstimate(
            flops=2 * rows * depth * width, bytes_accessed=2 * rows * (depth + width), transcendentals=0
        ),
    )(values, weight)


def head_specs(heads):
    def of(width, column):
        return pl.BlockSpec((2, 1, SEQ_MAX // 2, width), lambda b, h: (0, b, 0, column(h)))

    gain = pl.BlockSpec((1, HEAD), lambda b, h: (0, h))
    return of, [
        of(HEAD, lambda h: h),
        of(HEAD, lambda h: heads + h),
        of(HEAD, lambda h: 2 * heads + h),
        of(4, lambda h: 0),
        of(HEAD, lambda h: 0),
        of(HEAD, lambda h: 0),
        gain,
        gain,
        pl.BlockSpec((1, SEQ_MAX), lambda b, h: (0, 0)),
    ]


def in_blocks(array):
    return array.reshape(2, -1, SEQ_MAX // 2, array.shape[-1])


def attend(projected, info, cosine, sine, gain_q, gain_k, place):
    rows, columns = projected.shape[0], projected.shape[1] // 3
    heads, blocks = columns // HEAD, rows // SEQ_MAX
    of, specs = head_specs(heads)
    p = in_blocks(projected)
    mixed = pl.pallas_call(
        attend_kernel,
        grid=(blocks, heads),
        in_specs=specs,
        out_specs=of(HEAD, lambda h: h),
        out_shape=jax.ShapeDtypeStruct((2, blocks, SEQ_MAX // 2, columns), BF16),
        compiler_params=PARAMS,
        cost_estimate=pl.CostEstimate(
            flops=4 * rows * SEQ_MAX * columns, bytes_accessed=8 * rows * columns * 2, transcendentals=rows * SEQ_MAX * heads
        ),
    )(p, p, p, in_blocks(info), in_blocks(cosine), in_blocks(sine), gain_q, gain_k, place)
    return mixed.reshape(rows, columns)


def attend_back(projected, info, cosine, sine, gain_q, gain_k, place, mixed_grad):
    rows, columns = projected.shape[0], projected.shape[1] // 3
    heads, blocks = columns // HEAD, rows // SEQ_MAX
    of, specs = head_specs(heads)
    p = in_blocks(projected)
    shape = (2, blocks, SEQ_MAX // 2, columns)
    dq, dk, dv, means = pl.pallas_call(
        attend_back_kernel,
        grid=(blocks, heads),
        in_specs=specs + [of(HEAD, lambda h: h)],
        out_specs=[of(HEAD, lambda h: h)] * 3
        + [pl.BlockSpec((1, 2, 1, SEQ_MAX // 2, 2), lambda b, h: (h, 0, b, 0, 0))],
        out_shape=[
            jax.ShapeDtypeStruct(shape, F32),
            jax.ShapeDtypeStruct(shape, F32),
            jax.ShapeDtypeStruct(shape, BF16),
            jax.ShapeDtypeStruct((heads,) + shape[:3] + (2,), F32),
        ],
        scratch_shapes=[pltpu.VMEM((HEAD, SEQ_MAX), F32)] * 2 + [pltpu.VMEM((SEQ_MAX, HEAD), F32)],
        compiler_params=PARAMS,
        cost_estimate=pl.CostEstimate(
            flops=10 * rows * SEQ_MAX * columns, bytes_accessed=12 * rows * columns * 2, transcendentals=rows * SEQ_MAX * heads
        ),
    )(p, p, p, in_blocks(info), in_blocks(cosine), in_blocks(sine), gain_q, gain_k, place, in_blocks(mixed_grad))
    flat = [array.reshape(rows, columns) for array in (dq, dk, dv)]
    return *flat, jnp.sum(means, 0).reshape(rows, 2)


def qkv_grads(projected, dq, dk, dv, info, mean, gain_q, gain_k):
    rows, columns = dq.shape
    step = 512

    def by_row(width):
        return pl.BlockSpec((step, width), lambda i: (i, 0))

    def fixed(height):
        return pl.BlockSpec((height, columns), lambda i: (0, 0))

    return pl.pallas_call(
        qkv_grad_kernel,
        grid=(rows // step,),
        in_specs=[by_row(3 * columns)] + [by_row(columns)] * 3 + [by_row(4), by_row(2), fixed(1), fixed(1)],
        out_specs=[by_row(3 * columns), fixed(2)],
        out_shape=[
            jax.ShapeDtypeStruct((rows, 3 * columns), BF16),
            jax.ShapeDtypeStruct((2, columns), F32),
        ],
        compiler_params=PARAMS,
    )(projected, dq, dk, dv, info, mean, gain_q, gain_k)


def make_body(count, per_head):
    replicas = count // 8
    own_heads = replicas // per_head
    head_axes = GROUP[3 - int(math.log2(per_head)) :]
    head_shape = (per_head, own_heads, 8 // per_head)
    head_shape_put = (8 // per_head, per_head, own_heads)

    def body(
        tokens,
        cotangent,
        segment_ids,
        piece_ids,
        w_query,
        w_key,
        w_value,
        w_out,
        query_gain,
        key_gain,
        mixer_gain,
        w_gate,
        w_up,
        w_down,
        feed_gain,
    ):
        rows, width = tokens.shape
        weight_rows = w_query.shape[0]
        unit_rows = w_down.shape[0]
        units = replicas * unit_rows
        columns = own_heads * HEAD
        group_rows = 8 * rows
        blocks = group_rows // SEQ_MAX
        member = lax.axis_index(GROUP)
        device = lax.axis_index(ALL)

        def by_head(weight):
            shaped = weight.astype(BF16).reshape((weight_rows,) + head_shape + (HEAD,))
            return shaped.transpose(3, 1, 0, 2, 4).reshape(8, weight_rows, columns)

        def exchange(parts, group):
            return lax.all_to_all(parts, group, 0, 0, tiled=True)

        own_gains = jnp.stack([query_gain, key_gain, mixer_gain, feed_gain]).astype(BF16)
        qkv_parts = jnp.concatenate([by_head(w_query), by_head(w_key), by_head(w_value)], 2)
        qkv_piece = exchange(qkv_parts, GROUP).reshape(8 * weight_rows, 3 * columns)
        out_halves = gather_planes(w_out.astype(BF16))
        feed_parts = after(to_units(w_gate, w_up, unit_rows), qkv_piece, out_halves)
        feed_piece = exchange(feed_parts, GROUP).reshape(8 * weight_rows, 2 * units)
        plane_gains = doubled(after(own_gains, feed_piece).reshape(1, 4, weight_rows), PLANES)
        gains = doubled(plane_gains, GROUP).reshape(8, replicas, 4, weight_rows)
        gains = gains.transpose(2, 1, 0, 3).reshape(4, width).astype(F32)
        group_tokens = group_gather(after(tokens, feed_piece))
        weight_qkv = gather_planes(qkv_piece)
        weight_feed = gather_planes(feed_piece)
        weight_down = gather_planes(after(w_down.astype(BF16), feed_piece))
        out_halves = out_halves.reshape(per_head, own_heads, weight_rows, width)
        out_heads = lax.all_to_all(out_halves, head_axes, 0, 0, tiled=True)
        weight_out = out_heads.transpose(1, 0, 2, 3).reshape(columns, width)

        head_gains = gains[:2].reshape((2,) + head_shape + (HEAD,)).transpose(0, 3, 1, 2, 4)
        head_gains = lax.dynamic_index_in_dim(head_gains.reshape(2, 8, columns), member, 1, keepdims=False)
        gain_q, gain_k = head_gains.reshape(2, 1, columns)
        gain_a, gain_f = gains[2:3], gains[3:4]

        orders = [c + 4 * y + 2 * x for c in (0, 1) for y in (0, 1) for x in (0, 1)]
        starts = [(device ^ k) * rows for k in orders]

        def of_group(ids):
            return jnp.concatenate([lax.dynamic_slice_in_dim(ids, s, rows, 0) for s in starts])

        places = jnp.concatenate([s + jnp.arange(rows, dtype=jnp.int32) for s in starts])

        def by_block(array):
            shaped = array.reshape((2, blocks, group_rows // (2 * blocks)) + array.shape[1:])
            return jnp.moveaxis(shaped, 1, 0).reshape((blocks, SEQ_MAX) + array.shape[1:])

        def from_block(array):
            shaped = array.reshape((blocks, 2, SEQ_MAX // 2) + array.shape[2:])
            return jnp.moveaxis(shaped, 0, 1).reshape((group_rows,) + array.shape[2:])

        segment = by_block(of_group(segment_ids))
        piece = by_block(of_group(piece_ids))
        place_block = by_block(places) % SEQ_MAX
        before = jnp.sum((segment[:, None, :] < segment[:, :, None]).astype(jnp.int32), -1)
        positions = from_block(place_block - before)
        in_piece = (piece[:, None, :] == piece[:, :, None]) & (piece[:, :, None] > 0)
        piece_end = jnp.max(jnp.where(in_piece, place_block[:, None, :] + 1, 0), -1)
        first_seen = from_block(before).astype(F32)
        end_seen = from_block(jnp.maximum(place_block + 1, piece_end)).astype(F32)
        place = place_block[:1].astype(F32)
        freqs = jnp.exp(jnp.arange(HEAD // 2, dtype=F32) * (-2.0 * math.log(ROPE_BASE) / HEAD))
        angles = positions.astype(F32)[:, None] * freqs[None, :]
        cosine = jnp.concatenate([jnp.cos(angles), jnp.cos(angles)], 1)
        sine = jnp.concatenate([-jnp.sin(angles), jnp.sin(angles)], 1)

        projected = matmul(group_tokens, weight_qkv)
        squares = [jnp.sum(jnp.square(projected[:, i * columns : (i + 1) * columns]), -1) for i in (0, 1)]
        inverse = lax.rsqrt(group_sum(jnp.stack(squares)) / width + NORM_EPS)
        inverse = after(inverse, weight_out)
        info = lax.optimization_barrier(jnp.stack([first_seen, end_seen, inverse[0], inverse[1]], 1))
        attention = (projected, info, cosine, sine, gain_q, gain_k, place)

        def mix(attention, weight_out):
            mixed_low = attend(*attention)
            branch = group_scatter(*by_core(matmul, mixed_low, weight_out))
            hidden_in = tokens.astype(F32) + branch * inverse_rms(branch) * gain_a
            return mixed_low, branch, hidden_in, group_gather(hidden_in.astype(BF16))

        mixed_low, branch, hidden_in, group_hidden_in = region(mix, segment_ids, attention, weight_out)
        r_a = inverse_rms(branch)
        both, hidden = gate_up(group_hidden_in, weight_feed)
        result = group_scatter(*by_core(matmul, hidden, weight_down))
        r_m = inverse_rms(result)
        out_tokens = (hidden_in + result * r_m * gain_f).astype(BF16)

        def norm_back(values, r, gain, grad):
            scaled = gain * grad
            mean = jnp.mean(scaled * values, -1, keepdims=True)
            return r * (scaled - values * (r * r) * mean), jnp.sum(grad * values * r, 0)

        grad_out = cotangent.astype(F32)
        result_grad, feed_gain_term = norm_back(result, r_m, gain_f, grad_out)
        group_result_grad = group_gather(result_grad.astype(BF16))

        down_term = inner_t(hidden, group_result_grad).astype(BF16)
        down_share = scatter_planes(down_term)

        def feed_mix(group_result_grad, weight_down, weight_feed, both, group_hidden_in):
            feed_grad = gate_up_back(group_result_grad, weight_down, both)
            half = group_rows // 2
            for_other = times_transposed(feed_grad, weight_feed, half, half)
            arrived = swap(for_other, "c")
            for_mine = times_transposed(after(feed_grad, for_other), weight_feed, 0, half)
            sums = core_sum(for_mine, arrived)
            sends = lax.optimization_barrier(scatter_sends(sums))
            feed_term = inner_t(group_hidden_in, after(feed_grad, *sends)).astype(BF16)
            return feed_term, *scatter_start(sums, sends, feed_term)

        feed_term, top, bottom = region(
            feed_mix, segment_ids, after(group_result_grad, down_term), weight_down, weight_feed, both, group_hidden_in
        )
        feed_share = scatter_planes(feed_term)

        def to_mixer(top, bottom, branch, r_a):
            hidden_in_grad = grad_out + scatter_end(top, bottom)
            branch_grad, mixer_gain_term = norm_back(branch, r_a, gain_a, hidden_in_grad)
            return hidden_in_grad, mixer_gain_term, group_gather(branch_grad.astype(BF16))

        hidden_in_grad, mixer_gain_term, group_branch_grad = region(to_mixer, segment_ids, top, bottom, branch, r_a)
        group_branch_grad = after(group_branch_grad, down_share)
        mixed_grad = matmul_t(group_branch_grad, weight_out).astype(BF16)
        q_back, k_back, v_grad, means = attend_back(*attention, mixed_grad)
        means = group_sum(means.T).T / width
        grads, head_terms = qkv_grads(projected, q_back, k_back, v_grad, info, means, gain_q, gain_k)
        feed_back = exchange(after(feed_share, means).reshape(8, weight_rows, 2 * units), GROUP)
        qkv_term = inner_t(group_tokens, grads).astype(BF16)
        qkv_share = scatter_planes(qkv_term)
        out_term = inner_t(mixed_low, after(group_branch_grad, qkv_term, feed_share))
        out_parts = out_term.astype(BF16).reshape(own_heads, per_head, weight_rows, width)
        out_parts = lax.all_to_all(out_parts.transpose(1, 0, 2, 3), head_axes, 0, 0, tiled=True)
        out_share = scatter_planes(out_parts.reshape(replicas * weight_rows, width))

        head_terms = head_terms.reshape(2, 1, columns)
        spread = jnp.zeros((2, 8, columns), F32)
        spread = lax.dynamic_update_slice(spread, head_terms, (0, member, 0))
        spread = spread.reshape((2,) + head_shape_put + (HEAD,)).transpose(0, 2, 3, 1, 4)
        gain_terms = jnp.concatenate([spread.reshape(2, width), jnp.stack([mixer_gain_term, feed_gain_term])], 0)
        gain_terms = gain_terms.reshape(4, replicas, 8, weight_rows).transpose(2, 1, 0, 3)
        gain_terms = gain_terms.reshape(count, 4, weight_rows)

        def to_tokens(grads, weight_qkv, gain_terms, down_share, hidden_in_grad):
            mine, other = by_core(matmul_t, grads, weight_qkv)
            sums = core_sum(mine, swap(other, "c"))
            sends = scatter_sends(sums)
            done = halved(gain_terms, GROUP), down_share.astype(F32)
            return hidden_in_grad + scatter_end(*scatter_start(sums, sends, *done)), *done

        g_tokens, gain_terms, g_w_down = region(
            to_tokens, segment_ids, after(grads, out_parts), weight_qkv, gain_terms, down_share, hidden_in_grad
        )
        g_gains = halved(gain_terms, PLANES)[0]
        qkv_back = exchange(after(qkv_share, g_tokens, feed_back).reshape(8, weight_rows, 3 * columns), GROUP)
        heads_of = [
            [(e * own_heads + j) * (8 // per_head) + t for j in range(own_heads)]
            for t in range(8 // per_head)
            for e in range(per_head)
        ]
        g_qkv = from_heads(qkv_back, heads_of)
        g_w_out = out_share.astype(F32)
        g_w_gate, g_w_up = from_units(after(feed_back, g_tokens), unit_rows)

        return (
            out_tokens,
            g_tokens,
            g_qkv[0],
            g_qkv[1],
            g_qkv[2],
            g_w_out,
            g_gains[0],
            g_gains[1],
            g_gains[2],
            g_w_gate,
            g_w_up,
            g_w_down,
            g_gains[3],
        )

    return body


def solution(mesh):
    count = mesh.shape["dev"]
    grid = Mesh(mesh.devices.reshape(count // 16, 2, 2, 2, 2), ALL)

    def run(tokens, cotangent, segment_ids, piece_ids, w_query, *rest):
        per_head = count * HEAD // w_query.shape[0]
        rows, whole, gain = P(ALL, None), P(), P(ALL)
        in_specs = (rows, rows, whole, whole) + (rows,) * 4 + (gain,) * 3 + (rows,) * 3 + (gain,)
        out_specs = (rows,) * 6 + (gain,) * 3 + (rows,) * 3 + (gain,)
        return jax.shard_map(
            make_body(count, per_head), mesh=grid, in_specs=in_specs, out_specs=out_specs, check_vma=False
        )(tokens, cotangent, segment_ids, piece_ids, w_query, *rest)

    return run
```

```python
import math

import jax
import jax.numpy as jnp
from jax import lax
from jax.experimental import pallas as pl
from jax.experimental.pallas import tpu as pltpu
from jax.sharding import Mesh, PartitionSpec as P

HEAD = 128
SEQ_MAX = 1024
NORM_EPS = 1e-06
ROPE_BASE = 500000.0
MASKED = -1e30
BF16 = jnp.bfloat16
F32 = jnp.float32
GROUP = ("y", "x", "c")
ALL = ("zh", "zl", "y", "x", "c")
PLANES = ("zh", "zl")


def matmul(left, right):
    return jnp.dot(left, right, preferred_element_type=F32)


def matmul_t(left, right):
    return lax.dot_general(left, right, (((1,), (1,)), ((), ())), preferred_element_type=F32)


def inner_t(left, right):
    return lax.dot_general(left, right, (((0,), (0,)), ((), ())), preferred_element_type=F32)


def inverse_rms(values):
    return lax.rsqrt(jnp.mean(values * values, axis=-1, keepdims=True) + NORM_EPS)


def after(value, *others):
    return lax.optimization_barrier((value,) + others)[0]


def region(function, ids, *operands):
    def nothing(*operands):
        return jax.tree.map(lambda leaf: jnp.zeros(leaf.shape, leaf.dtype), jax.eval_shape(function, *operands))

    return lax.cond(ids[0] == 0, function, nothing, *operands)


def swap(block, axis):
    return lax.ppermute(block, axis, [(0, 1), (1, 0)])


def group_gather(own):
    half = own.shape[0] // 2
    near_x = swap(own, "x")
    near_y = swap(own, "y")
    top = swap(near_x[:half], "y")
    low = swap(near_y[half:], "x")
    first = jnp.concatenate([own, near_x, near_y], 0)
    blocks = lax.optimization_barrier(jnp.concatenate([first, own, swap(first, "c"), own], 0))
    last = jnp.concatenate([after(top, blocks), after(low, blocks)], 0)
    last_other = swap(last, "c")
    blocks = lax.dynamic_update_slice(blocks, last, (3 * 2 * half, 0))
    return lax.dynamic_update_slice(blocks, last_other, (7 * 2 * half, 0))


def group_sum(terms):
    total = terms.reshape(terms.shape[0], 2, 2, 2, -1)
    for dim, axis in enumerate(("c", "y", "x")):
        total = total + jnp.flip(swap(total, axis), dim + 1)
    return total.reshape(terms.shape)


def core_sum(mine, arrived):
    total = mine.astype(F32) + arrived.astype(F32)
    return total.astype(BF16).reshape(2, 2, 2, mine.shape[0] // 8, mine.shape[1])


def scatter_sends(sums):
    return sums[:, 1, 0], sums[1, :, 1]


def scatter_start(sums, sends, *others):
    got_x = after(swap(sends[0], "x"), *others)
    got_y = after(swap(sends[1], "y"), *others)
    return sums[:, 0, 0].astype(F32) + got_x.astype(F32), sums[0, :, 1].astype(F32) + got_y.astype(F32)


def scatter_end(top, bottom):
    top_last = swap(top[1].astype(BF16), "y")
    bottom_last = swap(bottom[1].astype(BF16), "x")
    return jnp.concatenate([top[0] + top_last.astype(F32), bottom[0] + bottom_last.astype(F32)], 0)


def group_scatter(mine, other):
    sums = core_sum(mine, swap(other, "c"))
    return scatter_end(*scatter_start(sums, scatter_sends(sums)))


def by_core(product, values, weight):
    half = values.shape[0] // 2
    other = product(values[half:], weight).astype(BF16)
    mine = product(after(values[:half], other), weight).astype(BF16)
    return lax.optimization_barrier(mine), other


def doubled(own, axes):
    for axis in reversed(axes):
        size = lax.axis_size(axis)
        step = 1
        while step < size:
            got = lax.ppermute(own, axis, [(i, i ^ step) for i in range(size)])
            low_side = lax.axis_index(axis) & step == 0
            own = jnp.concatenate([jnp.where(low_side, own, got), jnp.where(low_side, got, own)], 0)
            step *= 2
    return own


def halved(terms, axes):
    for axis in axes:
        size = lax.axis_size(axis)
        step = size // 2
        while step:
            low_side = lax.axis_index(axis) & step == 0
            first, second = jnp.split(terms, 2)
            got = lax.ppermute(
                jnp.where(low_side, second, first), axis, [(i, i ^ step) for i in range(size)]
            )
            terms = jnp.where(low_side, first, second) + got
            step //= 2
    return terms


def gather_planes(part):
    return lax.all_gather(part, PLANES, axis=0, tiled=True)


def scatter_planes(term):
    return lax.psum_scatter(term, PLANES, scatter_dimension=0, tiled=True)


SCALE = HEAD ** (-0.5)
ROWS = 256
FEED_ROWS = 512
PARAMS = pltpu.CompilerParams(vmem_limit_bytes=56 * 2**20)


def flat_rows(ref):
    return ref[...].reshape(-1, ref.shape[-1])


def turn(values, cosine, sine):
    return values * cosine + pltpu.roll(values, HEAD // 2, 1) * sine


def softmax_rows(query, key, place, info):
    scores = matmul_t(query, key) * SCALE
    visible = (place >= info[:, 0:1]) & (place < info[:, 1:2])
    masked = jnp.where(visible, scores, MASKED)
    weights = jnp.exp(masked - jnp.max(masked, -1, keepdims=True))
    return weights * (1.0 / jnp.sum(weights, -1, keepdims=True))


def attend_kernel(q_ref, k_ref, v_ref, info_ref, cos_ref, sin_ref, gq_ref, gk_ref, place_ref, o_ref):
    info, cosine, sine = flat_rows(info_ref), flat_rows(cos_ref), flat_rows(sin_ref)
    query = turn(flat_rows(q_ref) * info[:, 2:3] * gq_ref[...], cosine, sine).astype(BF16)
    key = turn(flat_rows(k_ref) * info[:, 3:4] * gk_ref[...], cosine, sine).astype(BF16)
    value = flat_rows(v_ref).astype(BF16)
    place = place_ref[...]
    for start in range(0, SEQ_MAX, ROWS):
        softmax = softmax_rows(query[start : start + ROWS], key, place, info[start : start + ROWS])
        mixed = matmul(softmax.astype(BF16), value).astype(BF16)
        half, at = divmod(start, SEQ_MAX // 2)
        o_ref[half, 0, at : at + ROWS] = mixed


def attend_back_kernel(
    q_ref, k_ref, v_ref, info_ref, cos_ref, sin_ref, gq_ref, gk_ref, place_ref, do_ref,
    dq_ref, dk_ref, dv_ref, mean_ref, dk_sum, dv_sum, dq_all,
):
    info, cosine, sine = flat_rows(info_ref), flat_rows(cos_ref), flat_rows(sin_ref)
    query_in, key_in = flat_rows(q_ref), flat_rows(k_ref)
    query = turn(query_in * info[:, 2:3] * gq_ref[...], cosine, sine).astype(BF16)
    key = turn(key_in * info[:, 3:4] * gk_ref[...], cosine, sine).astype(BF16)
    value = flat_rows(v_ref).astype(BF16)
    grad = flat_rows(do_ref)
    place = place_ref[...]
    for start in range(0, SEQ_MAX, ROWS):
        part = slice(start, start + ROWS)
        softmax = softmax_rows(query[part], key, place, info[part])
        softmax_grad = matmul_t(grad[part], value)
        inner = jnp.sum(softmax * softmax_grad, -1, keepdims=True)
        score_grad = (softmax * (softmax_grad - inner)).astype(BF16)
        dq_all[part] = matmul(score_grad, key) * SCALE
        dk_term = inner_t(query[part], score_grad)
        dv_term = inner_t(grad[part], softmax.astype(BF16))
        if start:
            dk_sum[...] += dk_term
            dv_sum[...] += dv_term
        else:
            dk_sum[...] = dk_term
            dv_sum[...] = dv_term
    dq = turn(dq_all[...], cosine, -sine)
    dk = turn(dk_sum[...].T * SCALE, cosine, -sine)
    dq_ref[...] = dq.reshape(dq_ref.shape)
    dk_ref[...] = dk.reshape(dk_ref.shape)
    dv_ref[...] = dv_sum[...].T.astype(BF16).reshape(dv_ref.shape)
    mean_q = jnp.sum(dq * gq_ref[...] * query_in, -1, keepdims=True)
    mean_k = jnp.sum(dk * gk_ref[...] * key_in, -1, keepdims=True)
    mean_ref[...] = jnp.concatenate([mean_q, mean_k], 1).reshape(mean_ref.shape)


def qkv_grad_kernel(p_ref, dq_ref, dk_ref, dv_ref, info_ref, mean_ref, gq_ref, gk_ref, grads_ref, gains_ref):
    columns = dq_ref.shape[1]
    info, mean = info_ref[...], mean_ref[...]
    terms = []
    for i, (d_ref, gain_ref) in enumerate(((dq_ref, gq_ref), (dk_ref, gk_ref))):
        values, r, d = p_ref[:, i * columns : (i + 1) * columns], info[:, 2 + i : 3 + i], d_ref[...]
        grad = r * (gain_ref[...] * d - values * (r * r) * mean[:, i : i + 1])
        grads_ref[:, i * columns : (i + 1) * columns] = grad.astype(BF16)
        terms.append(jnp.sum(d * values * r, 0, keepdims=True))
    grads_ref[:, 2 * columns :] = dv_ref[...]
    term = jnp.concatenate(terms, 0)

    @pl.when(pl.program_id(0) == 0)
    def _():
        gains_ref[...] = term

    @pl.when(pl.program_id(0) > 0)
    def _():
        gains_ref[...] += term


def to_units(gate, up, unit_rows):
    rows, width = gate.shape
    units = width // 8

    def kernel(gate_ref, up_ref, out_ref):
        for i, w_ref in enumerate((gate_ref, up_ref)):
            for m in range(8):
                for r in range(units // unit_rows):
                    source, target = (r * 8 + m) * unit_rows, i * units + r * unit_rows
                    out_ref[m, :, target : target + unit_rows] = w_ref[:, source : source + unit_rows].astype(BF16)

    step = min(rows, 16)
    return pl.pallas_call(
        kernel,
        grid=(rows // step,),
        in_specs=[pl.BlockSpec((step, width), lambda i: (i, 0))] * 2,
        out_specs=pl.BlockSpec((8, step, 2 * units), lambda i: (0, i, 0)),
        out_shape=jax.ShapeDtypeStruct((8, rows, 2 * units), BF16),
        compiler_params=PARAMS,
    )(gate, up)


def from_units(parts, unit_rows):
    _, rows, units = parts.shape
    units //= 2

    def kernel(p_ref, *out_refs):
        for i, out_ref in enumerate(out_refs):
            for m in range(8):
                for r in range(units // unit_rows):
                    target, source = (r * 8 + m) * unit_rows, i * units + r * unit_rows
                    out_ref[:, target : target + unit_rows] = p_ref[m, :, source : source + unit_rows].astype(F32)

    step = min(rows, 16)
    return pl.pallas_call(
        kernel,
        grid=(rows // step,),
        in_specs=[pl.BlockSpec((8, step, 2 * units), lambda i: (0, i, 0))],
        out_specs=[pl.BlockSpec((step, 8 * units), lambda i: (i, 0))] * 2,
        out_shape=[jax.ShapeDtypeStruct((rows, 8 * units), F32)] * 2,
        compiler_params=PARAMS,
    )(parts)


def from_heads(parts, members):
    _, rows, columns = parts.shape
    columns //= 3

    def kernel(p_ref, *out_refs):
        for i, out_ref in enumerate(out_refs):
            for m, targets in enumerate(members):
                for j, head in enumerate(targets):
                    source = i * columns + j * HEAD
                    out_ref[:, head * HEAD : (head + 1) * HEAD] = p_ref[m, :, source : source + HEAD].astype(F32)

    step = min(rows, 16)
    return pl.pallas_call(
        kernel,
        grid=(rows // step,),
        in_specs=[pl.BlockSpec((8, step, 3 * columns), lambda i: (0, i, 0))],
        out_specs=[pl.BlockSpec((step, 8 * columns), lambda i: (i, 0))] * 3,
        out_shape=[jax.ShapeDtypeStruct((rows, 8 * columns), F32)] * 3,
        compiler_params=PARAMS,
    )(parts)


def whole(array):
    return pl.BlockSpec(array.shape, lambda i: (0, 0), pipeline_mode=pl.Buffered(1))


def by_rows(step, width):
    return pl.BlockSpec((step, width), lambda i: (i, 0))


def gate_up(values, weight):
    rows, depth = values.shape
    units = weight.shape[1] // 2

    def kernel(v_ref, w_ref, both_ref, hidden_ref):
        for c in range(0, units, 512):
            gate = matmul(v_ref[...], w_ref[:, c : c + 512])
            up = matmul(v_ref[...], w_ref[:, units + c : units + c + 512])
            both_ref[:, c : c + 512] = gate
            both_ref[:, units + c : units + c + 512] = up
            hidden_ref[:, c : c + 512] = (gate / (1.0 + jnp.exp(-gate)) * up).astype(BF16)

    return pl.pallas_call(
        kernel,
        grid=(rows // ROWS,),
        in_specs=[by_rows(ROWS, depth), whole(weight)],
        out_specs=[by_rows(ROWS, 2 * units), by_rows(ROWS, units)],
        out_shape=[jax.ShapeDtypeStruct((rows, 2 * units), F32), jax.ShapeDtypeStruct((rows, units), BF16)],
        compiler_params=PARAMS,
        cost_estimate=pl.CostEstimate(
            flops=4 * rows * depth * units, bytes_accessed=14 * rows * units, transcendentals=rows * units
        ),
    )(values, weight)


def gate_up_back(grad, weight, both):
    rows, depth = grad.shape
    units = weight.shape[0]

    def kernel(g_ref, w_ref, both_ref, out_ref):
        for c in range(0, units, 512):
            hidden_grad = matmul_t(g_ref[...], w_ref[c : c + 512, :])
            gate, up = both_ref[:, c : c + 512], both_ref[:, units + c : units + c + 512]
            sig = 1.0 / (1.0 + jnp.exp(-gate))
            out_ref[:, c : c + 512] = (hidden_grad * up * sig * (1.0 + gate * (1.0 - sig))).astype(BF16)
            out_ref[:, units + c : units + c + 512] = (hidden_grad * (gate * sig)).astype(BF16)

    return pl.pallas_call(
        kernel,
        grid=(rows // FEED_ROWS,),
        in_specs=[by_rows(FEED_ROWS, depth), whole(weight), by_rows(FEED_ROWS, 2 * units)],
        out_specs=by_rows(FEED_ROWS, 2 * units),
        out_shape=jax.ShapeDtypeStruct((rows, 2 * units), BF16),
        compiler_params=PARAMS,
        cost_estimate=pl.CostEstimate(
            flops=2 * rows * depth * units, bytes_accessed=16 * rows * units, transcendentals=rows * units
        ),
    )(grad, weight, both)


def times_transposed(values, weight, first, rows):
    depth, width = values.shape[1], weight.shape[0]

    def kernel(v_ref, w_ref, out_ref):
        for c in range(0, width, 512):
            out_ref[:, c : c + 512] = matmul_t(v_ref[...], w_ref[c : c + 512, :]).astype(BF16)

    return pl.pallas_call(
        kernel,
        grid=(rows // FEED_ROWS,),
        in_specs=[pl.BlockSpec((FEED_ROWS, depth), lambda i: (first // FEED_ROWS + i, 0)), whole(weight)],
        out_specs=by_rows(FEED_ROWS, width),
        out_shape=jax.ShapeDtypeStruct((rows, width), BF16),
        compiler_params=PARAMS,
        cost_estimate=pl.CostEstimate(
            flops=2 * rows * depth * width, bytes_accessed=2 * rows * (depth + width), transcendentals=0
        ),
    )(values, weight)


def head_specs(heads):
    def of(width, column):
        return pl.BlockSpec((2, 1, SEQ_MAX // 2, width), lambda b, h: (0, b, 0, column(h)))

    gain = pl.BlockSpec((1, HEAD), lambda b, h: (0, h))
    return of, [
        of(HEAD, lambda h: h),
        of(HEAD, lambda h: heads + h),
        of(HEAD, lambda h: 2 * heads + h),
        of(4, lambda h: 0),
        of(HEAD, lambda h: 0),
        of(HEAD, lambda h: 0),
        gain,
        gain,
        pl.BlockSpec((1, SEQ_MAX), lambda b, h: (0, 0)),
    ]


def in_blocks(array):
    return array.reshape(2, -1, SEQ_MAX // 2, array.shape[-1])


def attend(projected, info, cosine, sine, gain_q, gain_k, place):
    rows, columns = projected.shape[0], projected.shape[1] // 3
    heads, blocks = columns // HEAD, rows // SEQ_MAX
    of, specs = head_specs(heads)
    p = in_blocks(projected)
    mixed = pl.pallas_call(
        attend_kernel,
        grid=(blocks, heads),
        in_specs=specs,
        out_specs=of(HEAD, lambda h: h),
        out_shape=jax.ShapeDtypeStruct((2, blocks, SEQ_MAX // 2, columns), BF16),
        compiler_params=PARAMS,
        cost_estimate=pl.CostEstimate(
            flops=4 * rows * SEQ_MAX * columns, bytes_accessed=8 * rows * columns * 2, transcendentals=rows * SEQ_MAX * heads
        ),
    )(p, p, p, in_blocks(info), in_blocks(cosine), in_blocks(sine), gain_q, gain_k, place)
    return mixed.reshape(rows, columns)


def attend_back(projected, info, cosine, sine, gain_q, gain_k, place, mixed_grad):
    rows, columns = projected.shape[0], projected.shape[1] // 3
    heads, blocks = columns // HEAD, rows // SEQ_MAX
    of, specs = head_specs(heads)
    p = in_blocks(projected)
    shape = (2, blocks, SEQ_MAX // 2, columns)
    dq, dk, dv, means = pl.pallas_call(
        attend_back_kernel,
        grid=(blocks, heads),
        in_specs=specs + [of(HEAD, lambda h: h)],
        out_specs=[of(HEAD, lambda h: h)] * 3
        + [pl.BlockSpec((1, 2, 1, SEQ_MAX // 2, 2), lambda b, h: (h, 0, b, 0, 0))],
        out_shape=[
            jax.ShapeDtypeStruct(shape, F32),
            jax.ShapeDtypeStruct(shape, F32),
            jax.ShapeDtypeStruct(shape, BF16),
            jax.ShapeDtypeStruct((heads,) + shape[:3] + (2,), F32),
        ],
        scratch_shapes=[pltpu.VMEM((HEAD, SEQ_MAX), F32)] * 2 + [pltpu.VMEM((SEQ_MAX, HEAD), F32)],
        compiler_params=PARAMS,
        cost_estimate=pl.CostEstimate(
            flops=10 * rows * SEQ_MAX * columns, bytes_accessed=12 * rows * columns * 2, transcendentals=rows * SEQ_MAX * heads
        ),
    )(p, p, p, in_blocks(info), in_blocks(cosine), in_blocks(sine), gain_q, gain_k, place, in_blocks(mixed_grad))
    flat = [array.reshape(rows, columns) for array in (dq, dk, dv)]
    return *flat, jnp.sum(means, 0).reshape(rows, 2)


def qkv_grads(projected, dq, dk, dv, info, mean, gain_q, gain_k):
    rows, columns = dq.shape
    step = 512

    def by_row(width):
        return pl.BlockSpec((step, width), lambda i: (i, 0))

    def fixed(height):
        return pl.BlockSpec((height, columns), lambda i: (0, 0))

    return pl.pallas_call(
        qkv_grad_kernel,
        grid=(rows // step,),
        in_specs=[by_row(3 * columns)] + [by_row(columns)] * 3 + [by_row(4), by_row(2), fixed(1), fixed(1)],
        out_specs=[by_row(3 * columns), fixed(2)],
        out_shape=[
            jax.ShapeDtypeStruct((rows, 3 * columns), BF16),
            jax.ShapeDtypeStruct((2, columns), F32),
        ],
        compiler_params=PARAMS,
    )(projected, dq, dk, dv, info, mean, gain_q, gain_k)


def make_body(count, per_head):
    replicas = count // 8
    own_heads = replicas // per_head
    head_axes = GROUP[3 - int(math.log2(per_head)) :]
    head_shape = (per_head, own_heads, 8 // per_head)
    head_shape_put = (8 // per_head, per_head, own_heads)

    def body(
        tokens,
        cotangent,
        segment_ids,
        piece_ids,
        w_query,
        w_key,
        w_value,
        w_out,
        query_gain,
        key_gain,
        mixer_gain,
        w_gate,
        w_up,
        w_down,
        feed_gain,
    ):
        rows, width = tokens.shape
        weight_rows = w_query.shape[0]
        unit_rows = w_down.shape[0]
        units = replicas * unit_rows
        columns = own_heads * HEAD
        group_rows = 8 * rows
        blocks = group_rows // SEQ_MAX
        member = lax.axis_index(GROUP)
        device = lax.axis_index(ALL)

        def by_head(weight):
            shaped = weight.astype(BF16).reshape((weight_rows,) + head_shape + (HEAD,))
            return shaped.transpose(3, 1, 0, 2, 4).reshape(8, weight_rows, columns)

        def exchange(parts, group):
            return lax.all_to_all(parts, group, 0, 0, tiled=True)

        own_gains = jnp.stack([query_gain, key_gain, mixer_gain, feed_gain]).astype(BF16)
        qkv_parts = jnp.concatenate([by_head(w_query), by_head(w_key), by_head(w_value)], 2)
        qkv_piece = exchange(qkv_parts, GROUP).reshape(8 * weight_rows, 3 * columns)
        out_halves = gather_planes(w_out.astype(BF16))
        feed_parts = after(to_units(w_gate, w_up, unit_rows), qkv_piece, out_halves)
        feed_piece = exchange(feed_parts, GROUP).reshape(8 * weight_rows, 2 * units)
        plane_gains = doubled(after(own_gains, feed_piece).reshape(1, 4, weight_rows), PLANES)
        gains = doubled(plane_gains, GROUP).reshape(8, replicas, 4, weight_rows)
        gains = gains.transpose(2, 1, 0, 3).reshape(4, width).astype(F32)
        group_tokens = group_gather(after(tokens, feed_piece))
        weight_qkv = gather_planes(qkv_piece)
        weight_feed = gather_planes(feed_piece)
        weight_down = gather_planes(after(w_down.astype(BF16), feed_piece))
        out_halves = out_halves.reshape(per_head, own_heads, weight_rows, width)
        out_heads = lax.all_to_all(out_halves, head_axes, 0, 0, tiled=True)
        weight_out = out_heads.transpose(1, 0, 2, 3).reshape(columns, width)

        head_gains = gains[:2].reshape((2,) + head_shape + (HEAD,)).transpose(0, 3, 1, 2, 4)
        head_gains = lax.dynamic_index_in_dim(head_gains.reshape(2, 8, columns), member, 1, keepdims=False)
        gain_q, gain_k = head_gains.reshape(2, 1, columns)
        gain_a, gain_f = gains[2:3], gains[3:4]

        orders = [c + 4 * y + 2 * x for c in (0, 1) for y in (0, 1) for x in (0, 1)]
        starts = [(device ^ k) * rows for k in orders]

        def of_group(ids):
            return jnp.concatenate([lax.dynamic_slice_in_dim(ids, s, rows, 0) for s in starts])

        places = jnp.concatenate([s + jnp.arange(rows, dtype=jnp.int32) for s in starts])

        def by_block(array):
            shaped = array.reshape((2, blocks, group_rows // (2 * blocks)) + array.shape[1:])
            return jnp.moveaxis(shaped, 1, 0).reshape((blocks, SEQ_MAX) + array.shape[1:])

        def from_block(array):
            shaped = array.reshape((blocks, 2, SEQ_MAX // 2) + array.shape[2:])
            return jnp.moveaxis(shaped, 0, 1).reshape((group_rows,) + array.shape[2:])

        segment = by_block(of_group(segment_ids))
        piece = by_block(of_group(piece_ids))
        place_block = by_block(places) % SEQ_MAX
        before = jnp.sum((segment[:, None, :] < segment[:, :, None]).astype(jnp.int32), -1)
        positions = from_block(place_block - before)
        in_piece = (piece[:, None, :] == piece[:, :, None]) & (piece[:, :, None] > 0)
        piece_end = jnp.max(jnp.where(in_piece, place_block[:, None, :] + 1, 0), -1)
        first_seen = from_block(before).astype(F32)
        end_seen = from_block(jnp.maximum(place_block + 1, piece_end)).astype(F32)
        place = place_block[:1].astype(F32)
        freqs = jnp.exp(jnp.arange(HEAD // 2, dtype=F32) * (-2.0 * math.log(ROPE_BASE) / HEAD))
        angles = positions.astype(F32)[:, None] * freqs[None, :]
        cosine = jnp.concatenate([jnp.cos(angles), jnp.cos(angles)], 1)
        sine = jnp.concatenate([-jnp.sin(angles), jnp.sin(angles)], 1)

        projected = matmul(group_tokens, weight_qkv)
        squares = [jnp.sum(jnp.square(projected[:, i * columns : (i + 1) * columns]), -1) for i in (0, 1)]
        inverse = lax.rsqrt(group_sum(jnp.stack(squares)) / width + NORM_EPS)
        inverse = after(inverse, weight_out)
        info = lax.optimization_barrier(jnp.stack([first_seen, end_seen, inverse[0], inverse[1]], 1))
        attention = (projected, info, cosine, sine, gain_q, gain_k, place)

        def mix(attention, weight_out):
            mixed_low = attend(*attention)
            branch = group_scatter(*by_core(matmul, mixed_low, weight_out))
            hidden_in = tokens.astype(F32) + branch * inverse_rms(branch) * gain_a
            return mixed_low, branch, hidden_in, group_gather(hidden_in.astype(BF16))

        mixed_low, branch, hidden_in, group_hidden_in = region(mix, segment_ids, attention, weight_out)
        r_a = inverse_rms(branch)
        both, hidden = gate_up(group_hidden_in, weight_feed)
        result = group_scatter(*by_core(matmul, hidden, weight_down))
        r_m = inverse_rms(result)
        out_tokens = (hidden_in + result * r_m * gain_f).astype(BF16)

        def norm_back(values, r, gain, grad):
            scaled = gain * grad
            mean = jnp.mean(scaled * values, -1, keepdims=True)
            return r * (scaled - values * (r * r) * mean), jnp.sum(grad * values * r, 0)

        grad_out = cotangent.astype(F32)
        result_grad, feed_gain_term = norm_back(result, r_m, gain_f, grad_out)
        group_result_grad = group_gather(result_grad.astype(BF16))

        down_term = inner_t(hidden, group_result_grad).astype(BF16)
        down_share = scatter_planes(down_term)

        def feed_mix(group_result_grad, weight_down, weight_feed, both, group_hidden_in):
            feed_grad = gate_up_back(group_result_grad, weight_down, both)
            half = group_rows // 2
            for_other = times_transposed(feed_grad, weight_feed, half, half)
            arrived = swap(for_other, "c")
            for_mine = times_transposed(after(feed_grad, for_other), weight_feed, 0, half)
            sums = core_sum(for_mine, arrived)
            sends = lax.optimization_barrier(scatter_sends(sums))
            feed_term = inner_t(group_hidden_in, after(feed_grad, *sends)).astype(BF16)
            return feed_term, *scatter_start(sums, sends, feed_term)

        feed_term, top, bottom = region(
            feed_mix, segment_ids, after(group_result_grad, down_term), weight_down, weight_feed, both, group_hidden_in
        )
        feed_share = scatter_planes(feed_term)

        def to_mixer(top, bottom, branch, r_a):
            hidden_in_grad = grad_out + scatter_end(top, bottom)
            branch_grad, mixer_gain_term = norm_back(branch, r_a, gain_a, hidden_in_grad)
            return hidden_in_grad, mixer_gain_term, group_gather(branch_grad.astype(BF16))

        hidden_in_grad, mixer_gain_term, group_branch_grad = region(to_mixer, segment_ids, top, bottom, branch, r_a)
        group_branch_grad = after(group_branch_grad, down_share)
        mixed_grad = matmul_t(group_branch_grad, weight_out).astype(BF16)
        q_back, k_back, v_grad, means = attend_back(*attention, mixed_grad)
        means = group_sum(means.T).T / width
        grads, head_terms = qkv_grads(projected, q_back, k_back, v_grad, info, means, gain_q, gain_k)
        feed_back = exchange(after(feed_share, means).reshape(8, weight_rows, 2 * units), GROUP)
        qkv_term = inner_t(group_tokens, grads).astype(BF16)
        qkv_share = scatter_planes(qkv_term)
        out_term = inner_t(mixed_low, after(group_branch_grad, qkv_term, feed_share))
        out_parts = out_term.astype(BF16).reshape(own_heads, per_head, weight_rows, width)
        out_parts = lax.all_to_all(out_parts.transpose(1, 0, 2, 3), head_axes, 0, 0, tiled=True)
        out_share = scatter_planes(out_parts.reshape(replicas * weight_rows, width))

        head_terms = head_terms.reshape(2, 1, columns)
        spread = jnp.zeros((2, 8, columns), F32)
        spread = lax.dynamic_update_slice(spread, head_terms, (0, member, 0))
        spread = spread.reshape((2,) + head_shape_put + (HEAD,)).transpose(0, 2, 3, 1, 4)
        gain_terms = jnp.concatenate([spread.reshape(2, width), jnp.stack([mixer_gain_term, feed_gain_term])], 0)
        gain_terms = gain_terms.reshape(4, replicas, 8, weight_rows).transpose(2, 1, 0, 3)
        gain_terms = gain_terms.reshape(count, 4, weight_rows)

        def to_tokens(grads, weight_qkv, gain_terms, down_share, hidden_in_grad):
            mine, other = by_core(matmul_t, grads, weight_qkv)
            sums = core_sum(mine, swap(other, "c"))
            sends = scatter_sends(sums)
            done = halved(gain_terms, GROUP), down_share.astype(F32)
            return hidden_in_grad + scatter_end(*scatter_start(sums, sends, *done)), *done

        g_tokens, gain_terms, g_w_down = region(
            to_tokens, segment_ids, after(grads, out_parts), weight_qkv, gain_terms, down_share, hidden_in_grad
        )
        g_gains = halved(gain_terms, PLANES)[0]
        qkv_back = exchange(after(qkv_share, g_tokens, feed_back).reshape(8, weight_rows, 3 * columns), GROUP)
        heads_of = [
            [(e * own_heads + j) * (8 // per_head) + t for j in range(own_heads)]
            for t in range(8 // per_head)
            for e in range(per_head)
        ]
        g_qkv = from_heads(qkv_back, heads_of)
        g_w_out = out_share.astype(F32)
        g_w_gate, g_w_up = from_units(after(feed_back, g_tokens), unit_rows)

        return (
            out_tokens,
            g_tokens,
            g_qkv[0],
            g_qkv[1],
            g_qkv[2],
            g_w_out,
            g_gains[0],
            g_gains[1],
            g_gains[2],
            g_w_gate,
            g_w_up,
            g_w_down,
            g_gains[3],
        )

    return body


def solution(mesh):
    count = mesh.shape["dev"]
    grid = Mesh(mesh.devices.reshape(count // 16, 2, 2, 2, 2), ALL)

    def run(tokens, cotangent, segment_ids, piece_ids, w_query, *rest):
        per_head = count * HEAD // w_query.shape[0]
        rows, whole, gain = P(ALL, None), P(), P(ALL)
        in_specs = (rows, rows, whole, whole) + (rows,) * 4 + (gain,) * 3 + (rows,) * 3 + (gain,)
        out_specs = (rows,) * 6 + (gain,) * 3 + (rows,) * 3 + (gain,)
        return jax.shard_map(
            make_body(count, per_head), mesh=grid, in_specs=in_specs, out_specs=out_specs, check_vma=False
        )(tokens, cotangent, segment_ids, piece_ids, w_query, *rest)

    return run
```
